256 devices in a mesh: fsdp: 8 (over y, x_lo), ctx: 32 (over z, x_hi, core).
Axes of the slice: x: 4 (x_hi: 2, x_lo: 2; x = x_hi * 2 + x_lo), y: 4, z: 8, core: 2. Of those that a mesh axis runs over, the one named last changes fastest.
Arguments:
- tokens: bfloat16 [8, 8192, 2048], P('fsdp', 'ctx'), may hold values from -6 to 6
- zx_weight: bfloat16 [2048, 4096], P(None, ('fsdp', 'ctx')), may hold values from -0.125 to 0.125
- bc_weight: bfloat16 [2048, 512], P(None, ('fsdp', 'ctx')), may hold values from -0.01171875 to 0.01171875
- dt_weight: bfloat16 [2048, 64], replicated, may hold values from -0.125 to 0.125
- decay_rate: float32 [32], replicated, may hold values from 2.3193359e-05 to 0.067
- skip_gain: float32 [32], replicated, may hold values from 0.5 to 2
- norm_gain: float32 [2048], replicated, may hold values from 0.25 to 1.75
- out_weight: bfloat16 [2048, 2048], P(None, ('fsdp', 'ctx')), may hold values from -0.125 to 0.125
Outputs:
- mixed: bfloat16 [8, 8192, 2048], P('fsdp', 'ctx')
The draws below stay inside these ranges and needn't reach their ends.
All inputs are finite; a program needn't handle non-finite values.
Results may differ from the reference program's by a relative error of at most 0.0087.
Values may be sent and summed in bfloat16 or wider, within the bound.
A program may use at most 256 MiB of HBM per device.

```python
import math
import jax
import jax.numpy as jnp
from jax import lax

D = 2048
HEADS = 32
STATE = 128
BLOCK = 128
E = 2048
SEQLEN = 8192
BATCH = 8


def draw_decay_rate(key, part):
    key = jax.random.fold_in(key, 7)
    pick_key, fast_key, slow_key = jax.random.split(key, 3)
    fast_share = 0.5
    chosen = jax.random.uniform(pick_key, (HEADS,)) < fast_share
    fast_rate = jnp.exp(jax.random.uniform(fast_key, (HEADS,), minval=math.log(1.0 / 40.0), maxval=math.log(1.0 / 15.0)))
    slow_rate = jnp.exp(jax.random.uniform(slow_key, (HEADS,), minval=math.log(0.2), maxval=math.log(2.0))) / SEQLEN
    return jnp.where(chosen, fast_rate, slow_rate).astype(jnp.float32)


def level_of(own_key, extent, cuts, smallest, largest):
    factor_of, own = 1.0, jax.random.fold_in(own_key, 6)
    for dim, parts in cuts:
        steps = jnp.exp(jax.random.uniform(jax.random.fold_in(own, dim), (parts,), jnp.float32, smallest / len(cuts), largest / len(cuts)))
        factor_of = factor_of * jnp.repeat(steps, extent[dim] // parts).reshape([-1 if axis == dim else 1 for axis in range(len(extent))])
    return factor_of


def normal_values(stream_key, dims, scale, most, cuts=(), dtype=jnp.bfloat16):
    array = scale * jax.random.normal(stream_key, dims, jnp.float32)
    if cuts:
        array = array * level_of(stream_key, dims, cuts, -0.22, 0.18)
    return jnp.clip(array, -most, most).astype(dtype)


def setup_inputs(seed: int = 0) -> dict:
    streams_of = jax.random.split(jax.random.key(seed), 9)
    tokens = normal_values(streams_of[0], (BATCH, SEQLEN, D), 1.0, 6.0, ((0, 8), (1, 32)))
    zx_weight = normal_values(streams_of[1], (D, 2 * E), D ** -0.5, 0.125, ((1, 256),))
    bc_weight = normal_values(streams_of[2], (D, 4 * STATE), (D * STATE) ** -0.5, 0.01171875, ((1, 256),))
    dt_weight = normal_values(streams_of[3], (D, 2 * HEADS), D ** -0.5, 0.125)
    decay_rate = draw_decay_rate(jax.random.fold_in(streams_of[8], 71), 0)
    skip_gain = jnp.clip(jax.random.uniform(streams_of[5], (HEADS,), jnp.float32, 0.5, 2.0), 0.5, 2.0)
    norm_gain = jnp.clip(1.0 + 0.15 * jax.random.normal(streams_of[6], (E,), jnp.float32), 0.25, 1.75)
    out_weight = normal_values(streams_of[7], (E, D), E ** -0.5, 0.125, ((1, 256),))
    return {"tokens": tokens, "zx_weight": zx_weight, "bc_weight": bc_weight, "dt_weight": dt_weight, "decay_rate": decay_rate, "skip_gain": skip_gain, "norm_gain": norm_gain, "out_weight": out_weight}


def span_scan(inner, b_rows, c_rows, step_size, decay_rate):
    length = inner.shape[0]
    width = inner.shape[1]
    heads = decay_rate.shape[0]
    head_size = width // heads
    state_size = b_rows.shape[1]
    block_count = length // BLOCK
    inner_blocks = inner.reshape(block_count, BLOCK, heads, head_size)
    b_blocks = b_rows.reshape(block_count, BLOCK, state_size)
    c_blocks = c_rows.reshape(block_count, BLOCK, state_size)
    step_blocks = step_size.reshape(block_count, BLOCK, heads)
    positions = jnp.arange(BLOCK)
    strict_mask = positions[:, None] > positions[None, :]

    def advance(state, pieces):
        inner_now, b_now, c_now, step_now = pieces
        log_decay = jnp.cumsum(-step_now * decay_rate[None, :], axis=0)
        log_heads = log_decay.T
        step_heads = step_now.T
        log_end = log_heads[:, -1]
        intersection = jnp.dot(c_now, b_now.T, preferred_element_type=jnp.float32)
        log_gap = log_heads[:, :, None] - log_heads[:, None, :]
        decayed = jnp.exp(jnp.where(strict_mask[None], log_gap, -jnp.inf))
        weights = (intersection[None] * decayed * step_heads[:, None, :]).astype(jnp.bfloat16)
        inner_wide = inner_now.astype(jnp.float32)
        y_intra = jnp.einsum('hts,shp->thp', weights.astype(jnp.float32), inner_wide)
        factor = jnp.exp(log_end[None, :] - log_decay) * step_now
        scaled_inner = (factor[:, :, None] * inner_wide).astype(jnp.bfloat16)
        k_state = jnp.einsum('shp,sn->hpn', scaled_inner.astype(jnp.float32), b_now.astype(jnp.float32))
        rounded = lax.optimization_barrier(state.astype(jnp.bfloat16)).astype(jnp.float32)
        y_inter = jnp.exp(log_decay)[:, :, None] * jnp.einsum('tn,hpn->thp', c_now.astype(jnp.float32), rounded)
        new_state = jnp.exp(log_end)[:, None, None] * state + k_state
        return (new_state, y_intra + y_inter)
    start = jnp.zeros((heads, head_size, state_size), jnp.float32)
    _, outputs = lax.scan(advance, start, (inner_blocks, b_blocks, c_blocks, step_blocks))
    return outputs.reshape(length, width)

def reference(tokens, zx_weight, bc_weight, dt_weight, decay_rate, skip_gain, norm_gain, out_weight):

    def one_sequence(token_rows):
        zx_proj = jnp.dot(token_rows, zx_weight, preferred_element_type=jnp.float32).astype(jnp.bfloat16)
        bc_proj = jnp.dot(token_rows, bc_weight, preferred_element_type=jnp.float32).astype(jnp.bfloat16)
        dt_raw = jnp.dot(token_rows, dt_weight, preferred_element_type=jnp.float32).astype(jnp.bfloat16)
        width = zx_proj.shape[1] // 2
        heads = decay_rate.shape[0]
        state_size = bc_proj.shape[1] // 4
        gate = zx_proj[:, :width]
        inner = zx_proj[:, width:]
        dt_fwd = jax.nn.softplus(dt_raw[:, :heads].astype(jnp.float32))
        dt_bwd = jax.nn.softplus(dt_raw[:, heads:].astype(jnp.float32))
        fwd_b = bc_proj[:, :state_size]
        fwd_c = bc_proj[:, state_size:2 * state_size]
        bwd_b = bc_proj[:, 2 * state_size:3 * state_size]
        bwd_c = bc_proj[:, 3 * state_size:]
        y_fwd = span_scan(inner, fwd_b, fwd_c, dt_fwd, decay_rate)
        y_bwd = span_scan(inner[::-1], bwd_b[::-1], bwd_c[::-1], dt_bwd[::-1], decay_rate)[::-1]
        skip_cols = jnp.repeat(skip_gain, width // heads)
        total = y_fwd + y_bwd + skip_cols[None, :] * inner.astype(jnp.float32)
        gated = total * jax.nn.silu(gate.astype(jnp.float32))
        scale = lax.rsqrt(lax.optimization_barrier(jnp.mean(gated * gated, axis=-1, keepdims=True)) + 1e-05)
        normed = (gated * scale * norm_gain[None, :]).astype(jnp.bfloat16)
        return jnp.dot(normed, out_weight, preferred_element_type=jnp.float32).astype(jnp.bfloat16)
    return lax.map(one_sequence, tokens)
```

```python
import functools

import jax
import jax.numpy as jnp
from jax import lax
from jax.experimental import pallas as pl
from jax.experimental.pallas import tpu as pltpu
from jax.sharding import PartitionSpec as P

MESH = pl.DeviceIdType.MESH
F32 = jnp.float32
BF16 = jnp.bfloat16
BLOCK = 128
ROWS = 512
NBLK = ROWS // BLOCK
WIDE = 1024
VMEM_BYTES = 60 * 1024 * 1024


def coords():
    f = lax.axis_index("fsdp")
    c = lax.axis_index("ctx")
    y, xl = f // 2, f % 2
    z, xh, core = c // 4, (c // 2) % 2, c % 2
    return y, xl, z, xh, core


def dev(y, x, z, core):
    return (y * 2 + x % 2, z * 4 + (x // 2) * 2 + core)


def dot_nt(a, b):
    return lax.dot_general(a, b, (((1,), (1,)), ((), ())), preferred_element_type=F32)


def dot_tn(a, b):
    return lax.dot_general(a, b, (((0,), (0,)), ((), ())), preferred_element_type=F32)


def dot_nn(a, b):
    return lax.dot_general(a, b, (((1,), (0,)), ((), ())), preferred_element_type=F32)


def parts3(v):
    hi = v.astype(BF16)
    r = v - hi.astype(F32)
    mid = r.astype(BF16)
    lo = (r - mid.astype(F32)).astype(BF16)
    return hi, mid, lo


def wait_bytes(ref, sem):
    pltpu.make_async_copy(ref, ref, sem).wait()


class Spread:
    def __init__(self, view, slot, send, recv):
        self.view, self.slot, self.send, self.recv = view, slot, send, recv
        self.started = []

    def copy(self, half, sy, sx, to, index):
        ref = self.view(half, sy, sx)
        c = pltpu.make_async_remote_copy(
            src_ref=ref,
            dst_ref=ref,
            send_sem=self.send.at[half, index],
            recv_sem=self.recv.at[half, index],
            device_id=to,
            device_id_type=MESH,
        )
        c.start()
        self.started.append(c)

    def begin(self):
        y, xl, z, xh, core = coords()
        x = xh * 2 + xl
        for k in (1, 3, 2):
            self.copy(0, self.slot(y), x, dev((y + k) % 4, x, z, core), k - 1)
            self.copy(1, self.slot(y), x, dev(y, (x + k) % 4, z, core), k - 1)
        for k in (1, 3, 2):
            self.copy(0, self.slot(y), x, dev(y, (x + k) % 4, z, core), 3 * k)
            self.copy(1, self.slot(y), x, dev((y + k) % 4, x, z, core), 3 * k)

    def forward(self):
        y, xl, z, xh, core = coords()
        x = xh * 2 + xl
        for j in (1, 3, 2):
            sy = self.slot((y - j) % 4)
            wait_bytes(self.view(0, sy, x), self.recv.at[0, j - 1])
            for k in (1, 3, 2):
                self.copy(0, sy, x, dev(y, (x + k) % 4, z, core), 12 + 3 * (k - 1) + j - 1)
            sx = (x - j) % 4
            wait_bytes(self.view(1, self.slot(y), sx), self.recv.at[1, j - 1])
            for k in (1, 3, 2):
                self.copy(1, self.slot(y), sx, dev((y + k) % 4, x, z, core), 12 + 3 * (k - 1) + j - 1)

    def arrivals(self):
        y, xl, z, xh, core = coords()
        x = xh * 2 + xl
        for j in (0, 1, 3, 2):
            for k in (1, 3, 2):
                index = 3 * k if j == 0 else 12 + 3 * (k - 1) + j - 1
                sy, sx = self.slot((y - j) % 4), (x - k) % 4
                wait_bytes(self.view(0, sy, sx), self.recv.at[0, index])
                yield 0, sy, sx
                sy, sx = self.slot((y - k) % 4), (x - j) % 4
                wait_bytes(self.view(1, sy, sx), self.recv.at[1, index])
                yield 1, sy, sx

    def drain(self):
        for c in self.started:
            c.wait_send()


def gather_kernel(
    zx, bc, ow, tok, wz, wb, wo, xs,
    bcs, ows, bcm, bcf, owm, owf,
    zsend, zrecv, bsend, brecv, osend, orecv, local,
    gs, gr, swap_s, swap_r,
):
    y, xl, z, xh, core = coords()
    x = xh * 2 + xl
    h, zc = z // 4, z % 4
    t, zl = zc // 2, zc % 2
    inner, yy = y // 2, y % 2
    ys = yy + 2 * t
    y_to = yy + 2 * ((t + 1 + inner) % 2)

    barrier = pltpu.get_barrier_semaphore()
    count = 0
    for dz in range(8):
        for dc in range(2):
            for dy in (0, 2):
                if (dz, dc, dy) != (0, 0, 0):
                    to = dev((y + dy) % 4, x, (z + dz) % 8, (core + dc) % 2)
                    pl.semaphore_signal(barrier, inc=1, device_id=to, device_id_type=MESH)
                    count += 1
    for k in (1, 3):
        pl.semaphore_signal(barrier, inc=1, device_id=dev((y + k) % 4, x, z, core), device_id_type=MESH)
        count += 1
    for k in (1, 2, 3):
        pl.semaphore_signal(barrier, inc=1, device_id=dev(y, (x + k) % 4, z, core), device_id_type=MESH)
        count += 1
    pl.semaphore_wait(barrier, count)

    def first(src, dst, to_y, send, recv):
        is_self = jnp.logical_and(to_y == y, h == core)
        for dz in (0, 1, 7, 2, 6, 3, 5, 4):
            c = pltpu.make_async_remote_copy(
                src_ref=src,
                dst_ref=dst,
                send_sem=send.at[dz],
                recv_sem=recv,
                device_id=dev(to_y, x, (z + dz) % 8, h),
                device_id_type=MESH,
            )
            if dz:
                c.start()
            else:

                @pl.when(is_self)
                def _():
                    pltpu.make_async_copy(src, dst, recv).start()

                @pl.when(jnp.logical_not(is_self))
                def _():
                    c.start()

        def done():
            for dz in range(8):
                if dz:
                    wait_bytes(src, send.at[dz])
                else:

                    @pl.when(jnp.logical_not(is_self))
                    def _():
                        wait_bytes(src, send.at[0])

        return done

    def own_z(g, sy, sl, src_core):
        return wz.at[g, sy, xl, sl, xh, pl.ds(src_core * 16, 16)]

    dones = [
        first(bc, bcs.at[zc, core], y, bsend, brecv.at[zc, core]),
        first(zx, own_z(inner, ys, zl, core), y_to, zsend, zrecv.at[inner, zl, core]),
        first(ow, ows.at[zc, core], y, osend, orecv.at[zc, core]),
    ]
    partner = dev(y, x, z, 1 - core)
    tok_own = pltpu.make_async_copy(tok, xs.at[core], local.at[0])
    tok_own.start()
    tok_far = pltpu.make_async_remote_copy(
        src_ref=tok, dst_ref=xs.at[core], send_sem=swap_s.at[0], recv_sem=swap_r.at[0],
        device_id=partner, device_id_type=MESH,
    )
    tok_far.start()

    for q in range(4):
        for s in range(2):
            wait_bytes(bcs.at[q, s], brecv.at[q, s])
    for q in range(4):
        for s in range(2):
            v = bcs[q, s].astype(F32)
            for j in range(8):
                bcf[4 * q + 2 * s : 4 * q + 2 * s + 2, 256 * j : 256 * j + 256] = v[2 * j : 2 * j + 2, :]
    bcm[...] = bcf[...].astype(BF16)
    put = pltpu.make_async_copy(bcm, wb.at[y, core, xl, xh], local.at[1])
    put.start()
    put.wait()

    def view_b(half, sy, sx):
        return wb.at[sy, core, sx % 2, sx // 2, :, pl.ds(1024 * half, 1024)]

    def view_g(g):
        return lambda half, sy, sx: wz.at[g, sy, sx % 2, half, sx // 2]

    def view_o(half, sy, sx):
        return wo.at[sy, sx % 2, core, pl.ds(2 * half, 2), sx // 2]

    same = lambda v: v
    flip = lambda v: (v + 2) % 4
    set_b = Spread(view_b, same, gs.at[0], gr.at[0])
    set_i = Spread(view_g(1), same, gs.at[1], gr.at[1])
    set_g = Spread(view_g(0), flip, gs.at[2], gr.at[2])
    set_o = Spread(view_o, same, gs.at[3], gr.at[3])

    set_b.begin()
    for s in range(2):
        for r in range(2):
            wait_bytes(own_z(1, y, s, r), zrecv.at[1, s, r])
    set_i.begin()
    set_b.forward()
    set_i.forward()

    for q in range(4):
        for s in range(2):
            wait_bytes(ows.at[q, s], orecv.at[q, s])
    for q in range(4):
        for s in range(2):
            v = ows[q, s].astype(F32)
            for j in range(2):
                owf[q, 8 * s : 8 * s + 8, 1024 * j : 1024 * j + 1024] = v[8 * j : 8 * j + 8, :]
    owm[...] = owf[...].astype(BF16)
    put = pltpu.make_async_copy(owm, wo.at[y, xl, core, :, xh], local.at[2])
    put.start()
    put.wait()
    for s in range(2):
        for r in range(2):
            wait_bytes(own_z(0, flip(y), s, r), zrecv.at[0, s, r])

    def swap(ref, index):
        c = pltpu.make_async_remote_copy(
            src_ref=ref, dst_ref=ref, send_sem=swap_s.at[index], recv_sem=swap_r.at[index],
            device_id=partner, device_id_type=MESH,
        )
        c.start()
        return c

    set_g.begin()
    set_o.begin()
    for _ in set_b.arrivals():
        pass
    swaps = [swap(wb.at[:, core], 1)]
    for _ in set_i.arrivals():
        pass
    set_g.forward()
    set_o.forward()
    for _ in set_g.arrivals():
        pass
    for _ in set_o.arrivals():
        pass
    swaps.append(swap(wo.at[:, :, core], 2))

    for done in dones:
        done()
    for s in (set_b, set_i, set_g, set_o):
        s.drain()
    tok_own.wait()
    tok_far.wait_send()
    wait_bytes(xs.at[1 - core], swap_r.at[0])
    for c in swaps:
        c.wait_send()
    wait_bytes(wb.at[:, 1 - core], swap_r.at[1])
    wait_bytes(wo.at[:, :, 1 - core], swap_r.at[2])


ANY = pl.BlockSpec(memory_space=pl.ANY)
INV = pl.BlockSpec(memory_space=pltpu.VMEM)


def gather(zx, bc, ow, tok):
    dma = pltpu.SemaphoreType.DMA
    return pl.pallas_call(
        gather_kernel,
        out_shape=(
            jax.ShapeDtypeStruct((2, 4, 2, 2, 2, 32, 2048), BF16),
            jax.ShapeDtypeStruct((4, 2, 2, 2, 16, 2048), BF16),
            jax.ShapeDtypeStruct((4, 2, 2, 4, 2, 16, 2048), BF16),
            jax.ShapeDtypeStruct((2, 256, 2048), BF16),
        ),
        in_specs=[ANY] * 4,
        out_specs=(ANY,) * 4,
        scratch_shapes=[
            pltpu.VMEM((4, 2, 16, 256), BF16),
            pltpu.VMEM((4, 2, 16, 1024), BF16),
            pltpu.VMEM((16, 2048), BF16),
            pltpu.VMEM((16, 2048), F32),
            pltpu.VMEM((4, 16, 2048), BF16),
            pltpu.VMEM((4, 16, 2048), F32),
            dma((8,)), dma((2, 2, 2)),
            dma((8,)), dma((4, 2)),
            dma((8,)), dma((4, 2)),
            dma((3,)),
            dma((4, 2, 21)), dma((4, 2, 21)),
            dma((3,)), dma((3,)),
        ],
        compiler_params=pltpu.CompilerParams(
            collective_id=0, has_side_effects=True, vmem_limit_bytes=VMEM_BYTES
        ),
        name="gather",
    )(zx, bc, ow, tok)


def head_map(lane, shape, axis):
    i = lax.broadcasted_iota(jnp.int32, shape, axis)
    zl, xl, yy, t = i % 2, (i // 2) % 2, (i // 4) % 2, (i // 8) % 2
    return (yy * 2 + xl) * 8 + lane * 4 + t * 2 + zl


def natural(lane, g):
    y, xl = g // 2, g % 2
    yy, t = y % 2, y // 2
    return ((yy * 2 + xl) * 8 + lane * 4 + t * 2) * 64


def widen(v):
    stacked = jnp.concatenate(parts3(v), axis=1)
    r = lax.broadcasted_iota(jnp.int32, (48, WIDE), 0)
    c = lax.broadcasted_iota(jnp.int32, (48, WIDE), 1)
    spread = (r % 16 == c // 64).astype(BF16)
    return dot_nn(stacked, spread)


def scan_kernel(x, wi, wb, dtw, decay, skip, inner, bco, lamo, kst, dend, pay, yo, dts, lamt):
    core = lax.axis_index("ctx") % 2
    xv = x[...].reshape(ROWS, 2048)
    bco[...] = dot_nt(xv, wb[...].reshape(512, 2048)).astype(BF16)
    for g in range(4):
        w = wi[0, g].reshape(256, 2048)
        inner[:, 256 * g : 256 * g + 256] = dot_nt(xv, w).astype(BF16)
    raw = dot_nt(xv, dtw[...]).astype(BF16)
    row = lax.broadcasted_iota(jnp.int32, (64, 32), 0)
    col = lax.broadcasted_iota(jnp.int32, (64, 32), 1)
    pick = row == head_map(core, (64, 32), 1) + 32 * (col // 16)
    v = dot_nn(raw, pick.astype(BF16))
    dt = jnp.maximum(v, 0.0) + jnp.log1p(jnp.exp(-jnp.abs(v)))
    dts[...] = dt

    def choose(ref):
        one = (lax.broadcasted_iota(jnp.int32, (32, 16), 0) == head_map(core, (32, 16), 1)).astype(BF16)
        return sum(dot_nn(p, one) for p in parts3(ref[...]))

    rate = choose(decay)
    gain = widen(choose(skip))
    rates = jnp.concatenate([rate, rate], axis=1)[:1]
    step = -dt * rates
    logdt = jnp.log(dt)
    r = lax.broadcasted_iota(jnp.int32, (BLOCK, BLOCK), 0)
    c = lax.broadcasted_iota(jnp.int32, (BLOCK, BLOCK), 1)
    lower = (c <= r).astype(BF16)
    upper = (c >= r).astype(BF16)
    fwd_col = lax.broadcasted_iota(jnp.int32, (BLOCK, 32), 1) < 16
    for b in range(NBLK):
        rows = slice(b * BLOCK, b * BLOCK + BLOCK)
        ps = parts3(step[rows])
        lam = jnp.where(fwd_col, sum(dot_nn(lower, p) for p in ps), sum(dot_nn(upper, p) for p in ps))
        lamo[rows, :] = lam
        padded = jnp.concatenate([lam - logdt[rows], jnp.zeros((BLOCK, 96), F32)], axis=1)
        lamt[b] = jnp.transpose(padded)[:32]

    for d in range(2):
        cols = slice(16 * d, 16 * d + 16)
        state = jnp.zeros((BLOCK, WIDE), F32)
        decays = jnp.ones((1, WIDE), F32)
        for b in range(NBLK) if d == 0 else reversed(range(NBLK)):
            rows = slice(b * BLOCK, b * BLOCK + BLOCK)
            lam = lamo[rows, cols]
            end = lam[BLOCK - 1 : BLOCK] if d == 0 else lam[0:1]
            factor = jnp.exp(end - lam) * dts[rows, cols]
            scaled = (widen(factor) * inner[rows, :].astype(F32)).astype(BF16)
            k = dot_tn(bco[rows, 256 * d : 256 * d + 128], scaled)
            de = widen(jnp.broadcast_to(jnp.exp(end), (8, 16)))[:1]
            dend[d, b] = de
            kst[d, b] = k
            state = de * state + k
            decays = decays * de
        for j in range(16):
            q, nh = j // 2, j % 2
            pay[j, 64 * d : 64 * d + 64, :] = state[64 * nh : 64 * nh + 64, 128 * q : 128 * q + 128].astype(BF16)
        if d == 0:
            decay_rows = list(parts3(decays))
        else:
            decay_rows = decay_rows + list(parts3(decays))
    tail = jnp.concatenate([p.astype(F32) for p in decay_rows] + [jnp.zeros((10, WIDE), F32)], axis=0).astype(BF16)
    for j in range(16):
        q = j // 2
        pay[j, 128:144, :] = tail[:, 128 * q : 128 * q + 128]

    left = lax.broadcasted_iota(jnp.int32, (BLOCK, BLOCK), 1) < 64

    def block(b, carry):
        rows = pl.ds(pl.multiple_of(b * BLOCK, BLOCK), BLOCK)
        gf = dot_nt(bco[rows, 128:256], bco[rows, 0:128])
        gb = dot_nt(bco[rows, 384:512], bco[rows, 256:384])
        g = jnp.where(r > c, gf, jnp.where(r < c, gb, 0.0))
        lam = lamo[rows, :]
        lt = lamt[b]
        for q in range(8):
            ws = []
            for i in range(2):
                lh = 2 * q + i
                gap_f = lam[:, lh : lh + 1] - lt[lh : lh + 1, :]
                gap_b = lam[:, 16 + lh : 17 + lh] - lt[16 + lh : 17 + lh, :]
                ws.append((g * jnp.exp(jnp.where(r > c, gap_f, gap_b))).astype(BF16))
            pair = inner[rows, 128 * q : 128 * q + 128]
            zero = jnp.zeros_like(pair)
            stack = jnp.concatenate([jnp.where(left, pair, zero), jnp.where(left, zero, pair)], axis=0)
            out = dot_nn(jnp.concatenate(ws, axis=1), stack)
            yo[rows, 128 * q : 128 * q + 128] = out + gain[:1, 128 * q : 128 * q + 128] * pair.astype(F32)
        return carry

    lax.fori_loop(0, NBLK, block, 0)


def local_scan(x, wz, wb, dtw, decay, skip):
    sd = jax.ShapeDtypeStruct
    return pl.pallas_call(
        scan_kernel,
        out_shape=(
            sd((ROWS, WIDE), BF16),
            sd((ROWS, 512), BF16),
            sd((ROWS, 32), F32),
            sd((2, NBLK, BLOCK, WIDE), F32),
            sd((2, NBLK, 1, WIDE), F32),
            sd((16, 144, 128), BF16),
            sd((ROWS, WIDE), F32),
        ),
        grid=(1,),
        in_specs=[
            INV,
            pl.BlockSpec((1, 4, 2, 2, 2, 32, 2048), lambda i: (1, 0, 0, 0, 0, 0, 0)),
            INV, INV, INV, INV,
        ],
        out_specs=(INV,) * 7,
        scratch_shapes=[pltpu.VMEM((ROWS, 32), F32), pltpu.VMEM((NBLK, 32, BLOCK), F32)],
        compiler_params=pltpu.CompilerParams(vmem_limit_bytes=VMEM_BYTES),
        name="scan",
    )(x, wz, wb, dtw, decay, skip)


def states_kernel(pay, out, got, reply, s1, r1, s2, r2):
    y, xl, z, xh, core = coords()
    me = z * 2 + xh

    def at(j):
        return dev(y, (j % 2) * 2 + xl, j // 2, core)

    barrier = pltpu.get_barrier_semaphore()
    for k in range(1, 16):
        pl.semaphore_signal(barrier, inc=1, device_id=at((me + k) % 16), device_id_type=MESH)
    pl.semaphore_wait(barrier, 15)

    def send(src, dst, ss, rs):
        cs = []
        for k in range(1, 16):
            j = (me + k) % 16
            c = pltpu.make_async_remote_copy(
                src_ref=src.at[j], dst_ref=dst.at[me], send_sem=ss.at[k - 1], recv_sem=rs.at[k - 1],
                device_id=at(j), device_id_type=MESH,
            )
            c.start()
            cs.append(c)
        dst[pl.ds(me, 1)] = src[pl.ds(me, 1)]
        for k in range(1, 16):
            wait_bytes(dst.at[(me - k) % 16], rs.at[k - 1])
        return cs

    cs = send(pay, got, s1, r1)
    for d in range(2):
        state = jnp.zeros((64, 128), F32)
        for i in range(16) if d == 0 else reversed(range(16)):
            reply[i, 64 * d : 64 * d + 64, :] = state.astype(BF16)
            ds = got[i, 128:144, :].astype(F32)
            decay = ds[3 * d : 3 * d + 1] + ds[3 * d + 1 : 3 * d + 2] + ds[3 * d + 2 : 3 * d + 3]
            state = decay * state + got[i, 64 * d : 64 * d + 64, :].astype(F32)
    cs += send(reply, out, s2, r2)
    for c in cs:
        c.wait_send()


def exchange_states(pay):
    dma = pltpu.SemaphoreType.DMA
    return pl.pallas_call(
        states_kernel,
        out_shape=jax.ShapeDtypeStruct((16, 128, 128), BF16),
        in_specs=[INV],
        out_specs=INV,
        scratch_shapes=[
            pltpu.VMEM((16, 144, 128), BF16),
            pltpu.VMEM((16, 128, 128), BF16),
            dma((15,)), dma((15,)), dma((15,)), dma((15,)),
        ],
        compiler_params=pltpu.CompilerParams(
            collective_id=1, has_side_effects=True, vmem_limit_bytes=VMEM_BYTES
        ),
        name="states",
    )(pay)


def finish_kernel(x, wg, bco, lamo, kst, dend, ent, yo, gain, out, sq, enter):
    core = lax.axis_index("ctx") % 2
    for q in range(8):
        cols = slice(128 * q, 128 * q + 128)
        for nh in range(2):
            piece = ent[2 * q + nh].astype(F32)
            enter[0, 64 * nh : 64 * nh + 64, cols] = piece[:64]
            enter[1, 64 * nh : 64 * nh + 64, cols] = piece[64:]
    total = [None] * NBLK
    for d in range(2):
        state = enter[d]
        for b in range(NBLK) if d == 0 else reversed(range(NBLK)):
            rows = slice(b * BLOCK, b * BLOCK + BLOCK)
            cv = bco[rows, 256 * d + 128 : 256 * d + 256]
            y = widen(jnp.exp(lamo[rows, 16 * d : 16 * d + 16])) * dot_nn(cv, state.astype(BF16))
            yo[rows, :] = yo[rows, :] + y
            state = dend[d, b] * state + kst[d, b]
    xv = x[...].reshape(ROWS, 2048)
    squares = jnp.zeros((ROWS, 1), F32)
    for g in range(4):
        gate = dot_nt(xv, wg[0, g].reshape(256, 2048)).astype(BF16).astype(F32)
        gated = yo[:, 256 * g : 256 * g + 256] * (gate / (1.0 + jnp.exp(-gate)))
        squares = squares + jnp.sum(gated * gated, axis=1, keepdims=True)
        for i in range(2):
            base = pl.multiple_of(natural(core, 2 * g + i), 128)
            cols = slice(256 * g + 128 * i, 256 * g + 128 * i + 128)
            out[:, cols] = (gated[:, 128 * i : 128 * i + 128] * gain[0:1, pl.ds(base, 128)]).astype(BF16)
    sq[...] = jnp.broadcast_to(squares, (ROWS, 128))


def finish(x, wz, bco, lamo, kst, dend, ent, yo, gain):
    return pl.pallas_call(
        finish_kernel,
        out_shape=(jax.ShapeDtypeStruct((ROWS, WIDE), BF16), jax.ShapeDtypeStruct((ROWS, 128), F32)),
        grid=(1,),
        in_specs=[
            INV,
            pl.BlockSpec((1, 4, 2, 2, 2, 32, 2048), lambda i: (0, 0, 0, 0, 0, 0, 0)),
            INV, INV, INV, INV, INV, INV, INV,
        ],
        out_specs=(INV, INV),
        scratch_shapes=[pltpu.VMEM((2, BLOCK, WIDE), F32)],
        compiler_params=pltpu.CompilerParams(vmem_limit_bytes=VMEM_BYTES),
        name="finish",
    )(x, wz, bco, lamo, kst, dend, ent, yo, gain)


def pair_kernel(g, sq, wide, sqo, far, farsq, ss, rs):
    y, xl, z, xh, core = coords()
    partner = dev(y, xh * 2 + xl, z, 1 - core)
    barrier = pltpu.get_barrier_semaphore()
    pl.semaphore_signal(barrier, inc=1, device_id=partner, device_id_type=MESH)
    pl.semaphore_wait(barrier, 1)
    theirs = pl.ds(pl.multiple_of((1 - core) * 256, 256), 256)
    mine = pl.ds(pl.multiple_of(core * 256, 256), 256)
    cs = []
    for i, (src, dst) in enumerate(((g.at[theirs], far), (sq.at[theirs], farsq))):
        c = pltpu.make_async_remote_copy(
            src_ref=src, dst_ref=dst, send_sem=ss.at[i], recv_sem=rs.at[i],
            device_id=partner, device_id_type=MESH,
        )
        c.start()
        cs.append(c)
    for i in range(8):
        wide[:, pl.ds(pl.multiple_of(natural(core, i), 128), 128)] = g[mine, 128 * i : 128 * i + 128]
    for c in cs:
        c.wait()
    for i in range(8):
        wide[:, pl.ds(pl.multiple_of(natural(1 - core, i), 128), 128)] = far[:, 128 * i : 128 * i + 128]
    sqo[...] = sq[mine, :] + farsq[...]


def exchange_pair(g, sq):
    dma = pltpu.SemaphoreType.DMA
    return pl.pallas_call(
        pair_kernel,
        out_shape=(jax.ShapeDtypeStruct((256, 2048), BF16), jax.ShapeDtypeStruct((256, 128), F32)),
        in_specs=[INV, INV],
        out_specs=(INV, INV),
        scratch_shapes=[
            pltpu.VMEM((256, WIDE), BF16),
            pltpu.VMEM((256, 128), F32),
            dma((2,)), dma((2,)),
        ],
        compiler_params=pltpu.CompilerParams(
            collective_id=2, has_side_effects=True, vmem_limit_bytes=VMEM_BYTES
        ),
        name="pair",
    )(g, sq)


def out_kernel(g, sq, wo, out):
    scale = lax.rsqrt(sq[:, :1] * (1.0 / 2048.0) + 1e-05)
    out[...] = (dot_nt(g[...], wo[...].reshape(256, 2048)) * scale).astype(BF16)


def project_out(g, sq, wo):
    return pl.pallas_call(
        out_kernel,
        out_shape=jax.ShapeDtypeStruct((256, 2048), BF16),
        grid=(8,),
        in_specs=[
            pl.BlockSpec((256, 2048), lambda i: (0, 0)),
            pl.BlockSpec((256, 128), lambda i: (0, 0)),
            pl.BlockSpec((1, 1, 2, 4, 2, 16, 2048), lambda i: (i // 2, i % 2, 0, 0, 0, 0, 0)),
        ],
        out_specs=pl.BlockSpec((256, 256), lambda i: (0, i)),
        compiler_params=pltpu.CompilerParams(vmem_limit_bytes=VMEM_BYTES),
        name="project_out",
    )(g, sq, wo)


def shards(tokens, zx_weight, bc_weight, dt_weight, decay_rate, skip_gain, norm_gain, out_weight):
    zx = zx_weight.T
    bc = bc_weight.T.reshape(2, 8, 256).transpose(1, 0, 2).reshape(16, 256)
    ow = out_weight.T.reshape(8, 2, 1024).transpose(1, 0, 2).reshape(16, 1024)
    wz, wb, wo, xs = gather(zx, bc, ow, tokens[0])
    decay = jnp.broadcast_to(decay_rate[None], (8, 32))
    skip = jnp.broadcast_to(skip_gain[None], (8, 32))
    inner, bco, lam, kst, dend, pay, yo = local_scan(xs, wz, wb, dt_weight.T, decay, skip)
    ent = exchange_states(pay)
    g, sq = finish(xs, wz, bco, lam, kst, dend, ent, yo, norm_gain[None])
    wide, sqs = exchange_pair(g, sq)
    return project_out(wide, sqs, wo)[None]


def solution(mesh):
    columns = P(None, ("fsdp", "ctx"))
    in_specs = (P("fsdp", "ctx", None), columns, columns, P(), P(), P(), P(), columns)
    return jax.shard_map(
        shards, mesh=mesh, in_specs=in_specs, out_specs=P("fsdp", "ctx", None), check_vma=False
    )
```

```python
import functools

import jax
import jax.numpy as jnp
from jax import lax
from jax.experimental import pallas as pl
from jax.experimental.pallas import tpu as pltpu
from jax.sharding import PartitionSpec as P

MESH = pl.DeviceIdType.MESH
F32 = jnp.float32
BF16 = jnp.bfloat16
BLOCK = 128
ROWS = 512
NBLK = ROWS // BLOCK
WIDE = 1024
VMEM_BYTES = 60 * 1024 * 1024


def coords():
    f = lax.axis_index("fsdp")
    c = lax.axis_index("ctx")
    y, xl = f // 2, f % 2
    z, xh, core = c // 4, (c // 2) % 2, c % 2
    return y, xl, z, xh, core


def dev(y, x, z, core):
    return (y * 2 + x % 2, z * 4 + (x // 2) * 2 + core)


def dot_nt(a, b):
    return lax.dot_general(a, b, (((1,), (1,)), ((), ())), preferred_element_type=F32)


def dot_tn(a, b):
    return lax.dot_general(a, b, (((0,), (0,)), ((), ())), preferred_element_type=F32)


def dot_nn(a, b):
    return lax.dot_general(a, b, (((1,), (0,)), ((), ())), preferred_element_type=F32)


def parts3(v):
    hi = v.astype(BF16)
    r = v - hi.astype(F32)
    mid = r.astype(BF16)
    lo = (r - mid.astype(F32)).astype(BF16)
    return hi, mid, lo


def wait_bytes(ref, sem):
    pltpu.make_async_copy(ref, ref, sem).wait()


class Ring:
    def __init__(self, view, slot, send, recv):
        self.view, self.slot, self.send, self.recv = view, slot, send, recv
        self.started = []

    def ref(self, half, j, m, part=None):
        y, xl, z, xh, core = coords()
        x = xh * 2 + xl
        dy, dx = (j, m) if half == 0 else (m, j)
        return self.view(half, self.slot((y - dy) % 4), (x - dx) % 4, part)

    def copy(self, half, ref, axis, step, index):
        y, xl, z, xh, core = coords()
        x = xh * 2 + xl
        to = dev((y + step) % 4, x, z, core) if axis == half else dev(y, (x + step) % 4, z, core)
        c = pltpu.make_async_remote_copy(
            src_ref=ref, dst_ref=ref, send_sem=self.send.at[half, index], recv_sem=self.recv.at[half, index],
            device_id=to, device_id_type=MESH,
        )
        c.start()
        self.started.append(c)

    def wait(self, half, ref, index):
        wait_bytes(ref, self.recv.at[half, index])

    def both(self, half, j):
        ref = self.ref(half, j, 0)
        self.copy(half, ref, 1, 1, 4 + 4 * j)
        self.copy(half, ref, 1, 3, 5 + 4 * j)

    def begin(self):
        for half in range(2):
            ref = self.ref(half, 0, 0)
            self.copy(half, ref, 0, 1, 0)
            self.copy(half, ref, 0, 3, 1)
        for half in range(2):
            self.both(half, 0)

    def turn(self, half, axis, base, block):
        self.wait(half, block(1), base)
        self.copy(half, block(1, 0), axis, 1, base + 2)
        self.wait(half, block(3), base + 1)
        self.copy(half, block(3, 1), axis, 3, base + 3)

    def first(self):
        for half in range(2):
            self.turn(half, 0, 0, lambda n, part=None: self.ref(half, n, 0, part))
        for half in range(2):
            self.both(half, 1)
            self.both(half, 3)

    def second(self):
        for half in range(2):
            for part in range(2):
                self.wait(half, self.ref(half, 2, 0, part), 2 + part)
            self.both(half, 2)

    def third(self, j):
        for half in range(2):
            self.turn(half, 1, 4 + 4 * j, lambda n, part=None: self.ref(half, j, n, part))

    def fourth(self, j):
        for half in range(2):
            for part in range(2):
                self.wait(half, self.ref(half, j, 2, part), 6 + 4 * j + part)

    def drain(self):
        for c in self.started:
            c.wait_send()


def head_map(lane, shape, axis):
    i = lax.broadcasted_iota(jnp.int32, shape, axis)
    zl, xl, yy, t = i % 2, (i // 2) % 2, (i // 4) % 2, (i // 8) % 2
    return (yy * 2 + xl) * 8 + lane * 4 + t * 2 + zl


def natural(lane, g):
    y, xl = g // 2, g % 2
    yy, t = y % 2, y // 2
    return pl.multiple_of(((yy * 2 + xl) * 8 + lane * 4 + t * 2) * 64, 128)


def widen(v):
    stacked = jnp.concatenate(parts3(v), axis=1)
    r = lax.broadcasted_iota(jnp.int32, (48, WIDE), 0)
    c = lax.broadcasted_iota(jnp.int32, (48, WIDE), 1)
    spread = (r % 16 == c // 64).astype(BF16)
    return dot_nn(stacked, spread)


def kernel(
    zx, bc, ow, tok, dtw, decay, skip, gain, result,
    wz, wb, wo, xs, bst, bstf, bcs, ows, bcm, bcf, owm, owf,
    inner, bco, lams, dts, lamt, wide_f, wide_l, wm, kst, dend, yo, enter,
    pay, got, reply, ent, gbuf, wide, sqb, sqf,
    zsend, zrecv, bsend, brecv, osend, orecv, local,
    gs, gr, swap_s, swap_r, s1, r1, s2, r2, ps, pr,
):
    y, xl, z, xh, core = coords()
    x = xh * 2 + xl
    h, zc = z // 4, z % 4
    t, zl = zc // 2, zc % 2
    inner_side, yy = y // 2, y % 2
    ys = yy + 2 * t
    y_to = yy + 2 * ((t + 1 + inner_side) % 2)
    chip = z * 2 + xh
    partner = dev(y, x, z, 1 - core)

    def state_peer(j):
        return dev(y, (j % 2) * 2 + xl, j // 2, core)

    def remote(src, dst, ss, rs, to):
        return pltpu.make_async_remote_copy(
            src_ref=src, dst_ref=dst, send_sem=ss, recv_sem=rs, device_id=to, device_id_type=MESH
        )

    barrier = pltpu.get_barrier_semaphore()
    peers = []
    for dz in range(8):
        for dc in range(2):
            for dy in (0, 2):
                if (dz, dc, dy) != (0, 0, 0):
                    peers.append(dev((y + dy) % 4, x, (z + dz) % 8, (core + dc) % 2))
        peers.append(dev(y, (x + 2) % 4, (z + dz) % 8, core))
    for k in (1, 3):
        peers.append(dev((y + k) % 4, x, z, core))
        peers.append(dev(y, (x + k) % 4, z, core))
    for to in peers:
        pl.semaphore_signal(barrier, inc=1, device_id=to, device_id_type=MESH)
    for j in range(8):
        bstf[2 * j : 2 * j + 2, :] = bc[:, 256 * j : 256 * j + 256].astype(F32)
    bst[...] = bstf[...].astype(BF16)
    pl.semaphore_wait(barrier, len(peers))

    def first(src, dst, to_y, send, recv):
        is_self = jnp.logical_and(to_y == y, h == core)
        for dz in (0, 1, 7, 2, 6, 3, 5, 4):
            c = remote(src, dst, send.at[dz], recv, dev(to_y, x, (z + dz) % 8, h))
            if dz:
                c.start()
            else:

                @pl.when(is_self)
                def _():
                    pltpu.make_async_copy(src, dst, recv).start()

                @pl.when(jnp.logical_not(is_self))
                def _():
                    c.start()

        def done():
            for dz in range(8):
                if dz:
                    wait_bytes(src, send.at[dz])
                else:

                    @pl.when(jnp.logical_not(is_self))
                    def _():
                        wait_bytes(src, send.at[0])

        return done

    def own_z(g, sy, sl, src_core):
        return wz.at[g, sy, xl, sl, xh, pl.ds(src_core * 16, 16)]

    dones = [
        first(bst, bcs.at[zc, core], y, bsend, brecv.at[zc, core]),
        first(zx, own_z(inner_side, ys, zl, core), y_to, zsend, zrecv.at[inner_side, zl, core]),
    ]
    tok_own = pltpu.make_async_copy(tok, xs.at[core], local.at[0])
    tok_own.start()
    tok_far = remote(tok, xs.at[core], swap_s.at[0], swap_r.at[0], partner)
    tok_far.start()
    dones.append(first(ow, ows.at[zc, core], y, osend, orecv.at[zc, core]))

    def view_b(half, sy, sx, part):
        lanes = pl.ds(1024 * half, 1024) if part is None else pl.ds(1024 * half + 512 * part, 512)
        return wb.at[sy, core, sx % 2, sx // 2, :, lanes]

    def view_g(g):
        def view(half, sy, sx, part):
            rows = pl.ds(0, 32) if part is None else pl.ds(16 * part, 16)
            return wz.at[g, sy, sx % 2, half, sx // 2, rows]

        return view

    def view_o(half, sy, sx, part):
        tiles = pl.ds(2 * half, 2) if part is None else pl.ds(2 * half + part, 1)
        return wo.at[sy, sx % 2, core, tiles, sx // 2]

    same = lambda v: v
    flip = lambda v: (v + 2) % 4
    set_b = Ring(view_b, same, gs.at[0], gr.at[0])
    set_i = Ring(view_g(1), same, gs.at[1], gr.at[1])
    set_g = Ring(view_g(0), flip, gs.at[2], gr.at[2])
    set_o = Ring(view_o, same, gs.at[3], gr.at[3])

    for q in range(4):
        for s in range(2):
            wait_bytes(bcs.at[q, s], brecv.at[q, s])
    for q in range(4):
        for s in range(2):
            v = bcs[q, s].astype(F32)
            for j in range(8):
                bcf[4 * q + 2 * s : 4 * q + 2 * s + 2, 256 * j : 256 * j + 256] = v[2 * j : 2 * j + 2, :]
    bcm[...] = bcf[...].astype(BF16)
    put = pltpu.make_async_copy(bcm, wb.at[y, core, xl, xh], local.at[1])
    put.start()
    put.wait()
    set_b.begin()
    for s in range(2):
        for r in range(2):
            wait_bytes(own_z(1, y, s, r), zrecv.at[1, s, r])
    set_i.begin()
    set_b.first()
    set_i.first()
    set_b.second()
    set_i.second()

    tok_own.wait()
    wait_bytes(xs.at[1 - core], swap_r.at[0])
    raw = dot_nt(xs[...].reshape(ROWS, 2048), dtw[...]).astype(BF16)
    row = lax.broadcasted_iota(jnp.int32, (64, 32), 0)
    col = lax.broadcasted_iota(jnp.int32, (64, 32), 1)
    pick = row == head_map(core, (64, 32), 1) + 32 * (col // 16)
    v = dot_nn(raw, pick.astype(BF16))
    dt = jnp.maximum(v, 0.0) + jnp.log1p(jnp.exp(-jnp.abs(v)))
    dts[...] = dt

    set_b.third(0)
    set_i.third(0)

    def choose(ref):
        one = (lax.broadcasted_iota(jnp.int32, (32, 16), 0) == head_map(core, (32, 16), 1)).astype(BF16)
        wide_ref = jnp.broadcast_to(ref[...], (8, 32))
        return sum(dot_nn(p, one) for p in parts3(wide_ref))

    rate = choose(decay)
    skips = widen(choose(skip))
    rates = jnp.concatenate([rate, rate], axis=1)[:1]
    step = -dt * rates
    logdt = jnp.log(dt)
    r = lax.broadcasted_iota(jnp.int32, (BLOCK, BLOCK), 0)
    c = lax.broadcasted_iota(jnp.int32, (BLOCK, BLOCK), 1)
    lower = (c <= r).astype(BF16)
    upper = (c >= r).astype(BF16)
    fwd_col = lax.broadcasted_iota(jnp.int32, (BLOCK, 32), 1) < 16
    for b in range(NBLK):
        rows = slice(b * BLOCK, b * BLOCK + BLOCK)
        sp = parts3(step[rows])
        lam = jnp.where(fwd_col, sum(dot_nn(lower, p) for p in sp), sum(dot_nn(upper, p) for p in sp))
        lams[rows, :] = lam
        padded = jnp.concatenate([lam - logdt[rows], jnp.zeros((BLOCK, 96), F32)], axis=1)
        lamt[b] = jnp.transpose(padded)[:32]

    set_b.third(1)
    set_b.third(3)
    set_i.third(1)
    set_i.third(3)
    set_b.third(2)
    set_i.third(2)
    for j in range(4):
        set_b.fourth(j)
    swaps = [remote(wb.at[:, core], wb.at[:, core], swap_s.at[1], swap_r.at[1], partner)]
    swaps[0].start()

    for d in range(2):
        cols = slice(16 * d, 16 * d + 16)
        for b in range(NBLK):
            rows = slice(b * BLOCK, b * BLOCK + BLOCK)
            lam = lams[rows, cols]
            end = lam[BLOCK - 1 : BLOCK] if d == 0 else lam[0:1]
            wide_f[d, rows, :] = widen(jnp.exp(end - lam) * dts[rows, cols])
            wl = widen(jnp.exp(lam))
            wide_l[d, rows, :] = wl
            dend[d, b] = wl[BLOCK - 1 : BLOCK] if d == 0 else wl[0:1]

    wait_bytes(wb.at[:, 1 - core], swap_r.at[1])
    bco[...] = dot_nt(xs[...].reshape(ROWS, 2048), wb[...].reshape(512, 2048)).astype(BF16)

    def block_weights(b, carry):
        rows = pl.ds(pl.multiple_of(b * BLOCK, BLOCK), BLOCK)
        gf = dot_nt(bco[rows, 128:256], bco[rows, 0:128])
        gb = dot_nt(bco[rows, 384:512], bco[rows, 256:384])
        g = jnp.where(r > c, gf, jnp.where(r < c, gb, 0.0))
        lam = lams[rows, :]
        lt = lamt[b]
        for lh in range(16):
            gap_f = lam[:, lh : lh + 1] - lt[lh : lh + 1, :]
            gap_b = lam[:, 16 + lh : 17 + lh] - lt[16 + lh : 17 + lh, :]
            w = g * jnp.exp(jnp.where(r > c, gap_f, gap_b))
            wm[b, :, 128 * lh : 128 * lh + 128] = w.astype(BF16)
        return carry

    lax.fori_loop(0, NBLK, block_weights, 0)

    for j in range(4):
        set_i.fourth(j)
    for q in range(4):
        for s in range(2):
            wait_bytes(ows.at[q, s], orecv.at[q, s])
    for q in range(4):
        for s in range(2):
            v = ows[q, s].astype(F32)
            for j in range(2):
                owf[q, 8 * s : 8 * s + 8, 1024 * j : 1024 * j + 1024] = v[8 * j : 8 * j + 8, :]
    owm[...] = owf[...].astype(BF16)
    put = pltpu.make_async_copy(owm, wo.at[y, xl, core, :, xh], local.at[2])
    put.start()
    for s in range(2):
        for q in range(2):
            wait_bytes(own_z(0, flip(y), s, q), zrecv.at[0, s, q])
    set_g.begin()
    put.wait()
    set_o.begin()

    for g in range(4):
        w = wz[1, g].reshape(256, 2048)
        inner[:, 256 * g : 256 * g + 256] = dot_nt(xs[...].reshape(ROWS, 2048), w).astype(BF16)

    decay_rows = []
    for d in range(2):
        state = jnp.zeros((BLOCK, WIDE), F32)
        decays = jnp.ones((1, WIDE), F32)
        for b in range(NBLK) if d == 0 else reversed(range(NBLK)):
            rows = slice(b * BLOCK, b * BLOCK + BLOCK)
            scaled = (wide_f[d, rows, :] * inner[rows, :].astype(F32)).astype(BF16)
            k = dot_tn(bco[rows, 256 * d : 256 * d + 128], scaled)
            de = dend[d, b]
            kst[d, b] = k
            state = de * state + k
            decays = decays * de
        for j in range(16):
            q, nh = j // 2, j % 2
            pay[j, 64 * d : 64 * d + 64, :] = state[64 * nh : 64 * nh + 64, 128 * q : 128 * q + 128].astype(BF16)
        decay_rows += list(parts3(decays))
    tail = jnp.concatenate([p.astype(F32) for p in decay_rows] + [jnp.zeros((10, WIDE), F32)], axis=0).astype(BF16)
    for j in range(16):
        q = j // 2
        pay[j, 128:144, :] = tail[:, 128 * q : 128 * q + 128]

    def send_states(src, dst, ss, rs):
        cs = []
        for k in range(1, 16):
            j = (chip + k) % 16
            c = remote(src.at[j], dst.at[chip], ss.at[k - 1], rs.at[k - 1], state_peer(j))
            c.start()
            cs.append(c)
        dst[pl.ds(chip, 1)] = src[pl.ds(chip, 1)]
        return cs

    def wait_states(dst, rs):
        for k in range(1, 16):
            wait_bytes(dst.at[(chip - k) % 16], rs.at[k - 1])

    state_copies = send_states(pay, got, s1, r1)
    set_g.first()
    set_o.first()

    left = lax.broadcasted_iota(jnp.int32, (BLOCK, BLOCK), 1) < 64

    def block_intra(b, carry):
        rows = pl.ds(pl.multiple_of(b * BLOCK, BLOCK), BLOCK)
        for q in range(8):
            pair = inner[rows, 128 * q : 128 * q + 128]
            zero = jnp.zeros_like(pair)
            stack = jnp.concatenate([jnp.where(left, pair, zero), jnp.where(left, zero, pair)], axis=0)
            out = dot_nn(wm[b, :, 256 * q : 256 * q + 256], stack)
            yo[rows, 128 * q : 128 * q + 128] = out + skips[:1, 128 * q : 128 * q + 128] * pair.astype(F32)
        return carry

    lax.fori_loop(0, NBLK, block_intra, 0)

    set_g.second()
    set_o.second()
    wait_states(got, r1)
    for d in range(2):
        state = jnp.zeros((64, 128), F32)
        for i in range(16) if d == 0 else reversed(range(16)):
            reply[i, 64 * d : 64 * d + 64, :] = state.astype(BF16)
            ds = got[i, 128:144, :].astype(F32)
            de = ds[3 * d : 3 * d + 1] + ds[3 * d + 1 : 3 * d + 2] + ds[3 * d + 2 : 3 * d + 3]
            state = de * state + got[i, 64 * d : 64 * d + 64, :].astype(F32)
    state_copies += send_states(reply, ent, s2, r2)

    for j in (0, 1, 3, 2):
        set_g.third(j)
        set_o.third(j)
    wait_states(ent, r2)
    for q in range(8):
        cols = slice(128 * q, 128 * q + 128)
        for nh in range(2):
            piece = ent[2 * q + nh].astype(F32)
            enter[0, 64 * nh : 64 * nh + 64, cols] = piece[:64]
            enter[1, 64 * nh : 64 * nh + 64, cols] = piece[64:]
    for d in range(2):
        state = enter[d]
        for b in range(NBLK) if d == 0 else reversed(range(NBLK)):
            rows = slice(b * BLOCK, b * BLOCK + BLOCK)
            cv = bco[rows, 256 * d + 128 : 256 * d + 256]
            yo[rows, :] = yo[rows, :] + wide_l[d, rows, :] * dot_nn(cv, state.astype(BF16))
            state = dend[d, b] * state + kst[d, b]

    for j in range(4):
        set_g.fourth(j)
    theirs = pl.ds(pl.multiple_of((1 - core) * 256, 256), 256)
    mine = pl.ds(pl.multiple_of(core * 256, 256), 256)
    squares = jnp.zeros((ROWS, 1), F32)
    pair_copies = []
    for g in range(4):
        w = wz[0, g].reshape(256, 2048)
        gate = dot_nt(xs[...].reshape(ROWS, 2048), w).astype(BF16).astype(F32)
        gated = yo[:, 256 * g : 256 * g + 256] * (gate / (1.0 + jnp.exp(-gate)))
        squares = squares + jnp.sum(gated * gated, axis=1, keepdims=True)
        for i in range(2 * g, 2 * g + 2):
            place = pl.ds(natural(core, i), 128)
            cols = slice(128 * i, 128 * i + 128)
            part = gated[:, 128 * (i % 2) : 128 * (i % 2) + 128]
            gbuf[:, cols] = (part * gain[0:1, place]).astype(BF16)
            cp = remote(gbuf.at[theirs, cols], wide.at[:, place], ps.at[i], pr.at[i], partner)
            cp.start()
            pair_copies.append(cp)
            wide[:, place] = gbuf[mine, cols]
    sqb[...] = jnp.broadcast_to(squares, (ROWS, 128))
    cp = remote(sqb.at[theirs], sqf, ps.at[8], pr.at[8], partner)
    cp.start()
    pair_copies.append(cp)

    for j in range(4):
        set_o.fourth(j)
    swaps.append(remote(wo.at[:, :, core], wo.at[:, :, core], swap_s.at[2], swap_r.at[2], partner))
    swaps[1].start()
    for i in range(8):
        wait_bytes(wide.at[:, pl.ds(natural(1 - core, i), 128)], pr.at[i])
    wait_bytes(sqf, pr.at[8])
    scale = lax.rsqrt((sqb[mine, :1] + sqf[:, :1]) * (1.0 / 2048.0) + 1e-05)
    wait_bytes(wo.at[:, :, 1 - core], swap_r.at[2])
    for g in range(8):
        w = wo[g // 2, g % 2].reshape(256, 2048)
        result[:, 256 * g : 256 * g + 256] = (dot_nt(wide[...], w) * scale).astype(BF16)

    for done in dones:
        done()
    for s in (set_b, set_i, set_g, set_o):
        s.drain()
    tok_far.wait_send()
    for cp in swaps + state_copies + pair_copies:
        cp.wait_send()


ANY = pl.BlockSpec(memory_space=pl.ANY)
INV = pl.BlockSpec(memory_space=pltpu.VMEM)


def layer(zx, bc, ow, tok, dtw, decay, skip, gain):
    dma = pltpu.SemaphoreType.DMA
    vm = pltpu.VMEM
    return pl.pallas_call(
        kernel,
        out_shape=jax.ShapeDtypeStruct((256, 2048), BF16),
        in_specs=[ANY, INV, ANY, ANY, INV, INV, INV, INV],
        out_specs=INV,
        scratch_shapes=[
            vm((2, 4, 2, 2, 2, 32, 2048), BF16), vm((4, 2, 2, 2, 16, 2048), BF16),
            vm((4, 2, 2, 4, 2, 16, 2048), BF16), vm((2, 256, 2048), BF16),
            vm((16, 256), BF16), vm((16, 256), F32),
            vm((4, 2, 16, 256), BF16), vm((4, 2, 16, 1024), BF16),
            vm((16, 2048), BF16), vm((16, 2048), F32), vm((4, 16, 2048), BF16), vm((4, 16, 2048), F32),
            vm((ROWS, WIDE), BF16), vm((ROWS, 512), BF16), vm((ROWS, 32), F32), vm((ROWS, 32), F32),
            vm((NBLK, 32, BLOCK), F32), vm((2, ROWS, WIDE), F32), vm((2, ROWS, WIDE), F32),
            vm((NBLK, BLOCK, 2048), BF16), vm((2, NBLK, BLOCK, WIDE), F32), vm((2, NBLK, 1, WIDE), F32),
            vm((ROWS, WIDE), F32), vm((2, BLOCK, WIDE), F32),
            vm((16, 144, 128), BF16), vm((16, 144, 128), BF16), vm((16, 128, 128), BF16),
            vm((16, 128, 128), BF16), vm((ROWS, WIDE), BF16), vm((256, 2048), BF16),
            vm((ROWS, 128), F32), vm((256, 128), F32),
            dma((8,)), dma((2, 2, 2)), dma((8,)), dma((4, 2)), dma((8,)), dma((4, 2)), dma((3,)),
            dma((4, 2, 20)), dma((4, 2, 20)), dma((3,)), dma((3,)),
            dma((15,)), dma((15,)), dma((15,)), dma((15,)), dma((9,)), dma((9,)),
        ],
        compiler_params=pltpu.CompilerParams(
            collective_id=0, has_side_effects=True, vmem_limit_bytes=VMEM_BYTES
        ),
        name="layer",
    )(zx, bc, ow, tok, dtw, decay, skip, gain)


def shards(tokens, zx_weight, bc_weight, dt_weight, decay_rate, skip_gain, norm_gain, out_weight):
    ow = out_weight.T.reshape(8, 2, 1024).transpose(1, 0, 2).reshape(16, 1024)
    return layer(
        zx_weight.T, bc_weight.T, ow, tokens[0], dt_weight.T,
        decay_rate[None], skip_gain[None], norm_gain[None],
    )[None]


def solution(mesh):
    columns = P(None, ("fsdp", "ctx"))
    in_specs = (P("fsdp", "ctx", None), columns, columns, P(), P(), P(), P(), columns)
    return jax.shard_map(
        shards, mesh=mesh, in_specs=in_specs, out_specs=P("fsdp", "ctx", None), check_vma=False
    )
```

```python
import functools

import jax
import jax.numpy as jnp
from jax import lax
from jax.experimental import pallas as pl
from jax.experimental.pallas import tpu as pltpu
from jax.sharding import PartitionSpec as P

MESH = pl.DeviceIdType.MESH
F32 = jnp.float32
BF16 = jnp.bfloat16
BLOCK = 128
ROWS = 512
NBLK = ROWS // BLOCK
WIDE = 1024
VMEM_BYTES = 60 * 1024 * 1024


def coords():
    f = lax.axis_index("fsdp")
    c = lax.axis_index("ctx")
    y, xl = f // 2, f % 2
    z, xh, core = c // 4, (c // 2) % 2, c % 2
    return y, xl, z, xh, core


def dev(y, x, z, core):
    return (y * 2 + x % 2, z * 4 + (x // 2) * 2 + core)


def dot_nt(a, b):
    return lax.dot_general(a, b, (((1,), (1,)), ((), ())), preferred_element_type=F32)


def dot_tn(a, b):
    return lax.dot_general(a, b, (((0,), (0,)), ((), ())), preferred_element_type=F32)


def dot_nn(a, b):
    return lax.dot_general(a, b, (((1,), (0,)), ((), ())), preferred_element_type=F32)


def parts3(v):
    hi = v.astype(BF16)
    r = v - hi.astype(F32)
    mid = r.astype(BF16)
    lo = (r - mid.astype(F32)).astype(BF16)
    return hi, mid, lo


def wait_bytes(ref, sem):
    pltpu.make_async_copy(ref, ref, sem).wait()


class Ring:
    def __init__(self, view, slot, send, recv):
        self.view, self.slot, self.send, self.recv = view, slot, send, recv
        self.started = []

    def ref(self, half, j, m, part=None):
        y, xl, z, xh, core = coords()
        x = xh * 2 + xl
        dy, dx = (j, m) if half == 0 else (m, j)
        return self.view(half, self.slot((y - dy) % 4), (x - dx) % 4, part)

    def copy(self, half, ref, axis, step, index):
        y, xl, z, xh, core = coords()
        x = xh * 2 + xl
        to = dev((y + step) % 4, x, z, core) if axis == half else dev(y, (x + step) % 4, z, core)
        c = pltpu.make_async_remote_copy(
            src_ref=ref, dst_ref=ref, send_sem=self.send.at[half, index], recv_sem=self.recv.at[half, index],
            device_id=to, device_id_type=MESH,
        )
        c.start()
        self.started.append(c)

    def wait(self, half, ref, index):
        wait_bytes(ref, self.recv.at[half, index])

    def both(self, half, j):
        ref = self.ref(half, j, 0)
        self.copy(half, ref, 1, 1, 4 + 4 * j)
        self.copy(half, ref, 1, 3, 5 + 4 * j)

    def begin(self):
        for half in range(2):
            ref = self.ref(half, 0, 0)
            self.copy(half, ref, 0, 1, 0)
            self.copy(half, ref, 0, 3, 1)
        for half in range(2):
            self.both(half, 0)

    def turn(self, half, axis, base, block):
        self.wait(half, block(1), base)
        self.copy(half, block(1, 0), axis, 1, base + 2)
        self.wait(half, block(3), base + 1)
        self.copy(half, block(3, 1), axis, 3, base + 3)

    def first(self):
        for half in range(2):
            self.turn(half, 0, 0, lambda n, part=None: self.ref(half, n, 0, part))
        for half in range(2):
            self.both(half, 1)
            self.both(half, 3)

    def second(self):
        for half in range(2):
            for part in range(2):
                self.wait(half, self.ref(half, 2, 0, part), 2 + part)
            self.both(half, 2)

    def third(self, j):
        for half in range(2):
            self.turn(half, 1, 4 + 4 * j, lambda n, part=None: self.ref(half, j, n, part))

    def fourth(self, j):
        for half in range(2):
            for part in range(2):
                self.wait(half, self.ref(half, j, 2, part), 6 + 4 * j + part)

    def drain(self):
        for c in self.started:
            c.wait_send()


def head_map(lane, shape, axis):
    i = lax.broadcasted_iota(jnp.int32, shape, axis)
    zl, xl, yy, t = i % 2, (i // 2) % 2, (i // 4) % 2, (i // 8) % 2
    return (yy * 2 + xl) * 8 + lane * 4 + t * 2 + zl


def natural(lane, g):
    y, xl = g // 2, g % 2
    yy, t = y % 2, y // 2
    return pl.multiple_of(((yy * 2 + xl) * 8 + lane * 4 + t * 2) * 64, 128)


def widen(v):
    stacked = jnp.concatenate(parts3(v), axis=1)
    r = lax.broadcasted_iota(jnp.int32, (48, WIDE), 0)
    c = lax.broadcasted_iota(jnp.int32, (48, WIDE), 1)
    spread = (r % 16 == c // 64).astype(BF16)
    return dot_nn(stacked, spread)


def kernel(
    zx, bc, ow, tok, dtw, decay, skip, gain, result,
    wz, wb, wo, xs, bst, bstf, bcs, ows, bcm, bcf, owm, owf,
    inner, bco, lams, dts, lamt, wide_f, wide_l, wm, kst, dend, yo, enter,
    pay, got, reply, ent, gbuf, wide, sqb, sqf,
    d0s, d0r, zs_s, zs_r, local, gs, gr, ozs, ozr, osw_s, osw_r,
    swap_s, swap_r, s1, r1, s2, r2, ps, pr,
):
    y, xl, z, xh, core = coords()
    x = xh * 2 + xl
    h, zc = z // 4, z % 4
    t, zl = zc // 2, zc % 2
    inner_side, yy = y // 2, y % 2
    ys = yy + 2 * t
    y_to = yy + 2 * ((t + 1 + inner_side) % 2)
    chip = z * 2 + xh
    partner = dev(y, x, z, 1 - core)

    def state_peer(j):
        return dev(y, (j % 2) * 2 + xl, j // 2, core)

    def remote(src, dst, ss, rs, to):
        return pltpu.make_async_remote_copy(
            src_ref=src, dst_ref=dst, send_sem=ss, recv_sem=rs, device_id=to, device_id_type=MESH
        )

    barrier = pltpu.get_barrier_semaphore()
    peers = [partner, dev((y + 2) % 4, x, z, core), dev((y + 2) % 4, x, z, 1 - core)]
    for k in (1, 3):
        peers.append(dev((y + k) % 4, x, z, core))
        peers.append(dev(y, (x + k) % 4, z, core))
    for k in (1, 7):
        peers.append(dev(y, x, (z + k) % 8, core))
    for k in range(1, 16):
        if k not in (2, 14):
            peers.append(state_peer((chip + k) % 16))
    for to in peers:
        pl.semaphore_signal(barrier, inc=1, device_id=to, device_id_type=MESH)
    for j in range(8):
        bstf[2 * j : 2 * j + 2, :] = bc[:, 256 * j : 256 * j + 256].astype(F32)
    bst[...] = bstf[...].astype(BF16)
    pl.semaphore_wait(barrier, len(peers))

    def own_z(g, sy, sl, src_core):
        return wz.at[g, sy, xl, sl, xh, pl.ds(src_core * 16, 16)]

    def home(src, dst, to_y, kind):
        is_self = jnp.logical_and(to_y == y, h == core)
        far = remote(src, dst, d0s.at[kind], d0r.at[kind, core], dev(to_y, x, z, h))

        @pl.when(is_self)
        def _():
            pltpu.make_async_copy(src, dst, d0r.at[kind, core]).start()

        @pl.when(jnp.logical_not(is_self))
        def _():
            far.start()

        def done():
            @pl.when(jnp.logical_not(is_self))
            def _():
                far.wait_send()

        return done

    dones = [
        home(bst, bcs.at[zc, core], y, 0),
        home(zx, own_z(inner_side, ys, zl, core), y_to, 1),
    ]
    merge = remote(ow, ows.at[core], swap_s.at[2], swap_r.at[2], partner)
    merge.start()
    merge_own = pltpu.make_async_copy(ow, ows.at[core], local.at[2])
    merge_own.start()
    tok_own = pltpu.make_async_copy(tok, xs.at[core], local.at[0])
    tok_own.start()
    tok_far = remote(tok, xs.at[core], swap_s.at[0], swap_r.at[0], partner)
    tok_far.start()

    def kept(zsrc):
        q = zsrc % 4
        side = 1 - (q // 2 + y // 2) % 2
        return q, bcs.at[q], wz.at[side, yy + 2 * (q // 2), xl, q % 2, xh]

    def hop(zsrc, d, way):
        q, b_ref, z_ref = kept(zsrc)
        mine_now = zsrc // 4 == core
        ways = (0, 1) if d == 0 else (way,) if d < (4 if way == 0 else 3) else ()
        out = []
        for w in ways:
            to = dev(y, x, (z + 1 + 6 * w) % 8, core)
            out.append(remote(b_ref, b_ref, zs_s.at[0, w, d], zs_r.at[0, q], to))
            out.append(remote(z_ref, z_ref, zs_s.at[1, w, d], zs_r.at[1, q], to))

        @pl.when(mine_now)
        def _():
            if d == 0:
                for s in range(2):
                    wait_bytes(bcs.at[q, s], d0r.at[0, s])
                for s in range(2):
                    wait_bytes(z_ref.at[pl.ds(16 * s, 16)], d0r.at[1, s])
            else:
                wait_bytes(b_ref, zs_r.at[0, q])
                wait_bytes(z_ref, zs_r.at[1, q])
            for cp in out:
                cp.start()

        def done():
            @pl.when(mine_now)
            def _():
                for cp in out:
                    cp.wait_send()

        dones.append(done)

    def hops(d):
        hop((z - d) % 8, d, 0)
        if 0 < d < 4:
            hop((z + d) % 8, d, 1)

    def view_b(half, sy, sx, part):
        lanes = pl.ds(1024 * half, 1024) if part is None else pl.ds(1024 * half + 512 * part, 512)
        return wb.at[sy, core, sx % 2, sx // 2, :, lanes]

    def view_g(g):
        def view(half, sy, sx, part):
            rows = pl.ds(0, 32) if part is None else pl.ds(16 * part, 16)
            return wz.at[g, sy, sx % 2, half, sx // 2, rows]

        return view

    my_lanes = pl.multiple_of(1024 * core, 1024)

    def view_o(half, sy, sx, part):
        lanes = pl.ds(my_lanes + 512 * half, 512) if part is None else pl.ds(my_lanes + 512 * half + 256 * part, 256)
        return wo.at[sy, sx % 2, z, sx // 2, :, lanes]

    def plane(zsrc, part):
        return wo.at[:, :, zsrc, :, :, pl.ds(my_lanes + 512 * part, 512)]

    o_copies = []

    def o_send(zsrc, way, d, part):
        ref = plane(zsrc, part)
        to = dev(y, x, (z + 1 + 6 * way) % 8, core)
        cp = remote(ref, ref, ozs.at[way, d, part], ozr.at[way, d, part], to)
        cp.start()
        o_copies.append(cp)

    def o_swap(zsrc, index):
        for part in range(2):
            ref = plane(zsrc, part)
            cp = remote(ref, ref, osw_s.at[index, part], osw_r.at[index, part], partner)
            cp.start()
            o_copies.append(cp)

    def o_turn(d):
        for way in range(2):
            zsrc = (z - d) % 8 if way == 0 else (z + d) % 8
            for part in range(2):
                if d < 4 or part == way:
                    wait_bytes(plane(zsrc, part), ozr.at[way, d - 1, part])
                if d < 3 or (d == 3 and part == way):
                    o_send(zsrc, way, d, part)
        for way in range(2):
            zsrc = (z - d) % 8 if way == 0 else (z + d) % 8
            if d < 4 or way == 0:
                o_swap(zsrc, d if way == 0 else 8 - d)

    same = lambda v: v
    flip = lambda v: (v + 2) % 4
    set_b = Ring(view_b, same, gs.at[0], gr.at[0])
    set_i = Ring(view_g(1), same, gs.at[1], gr.at[1])
    set_g = Ring(view_g(0), flip, gs.at[2], gr.at[2])
    set_o = Ring(view_o, same, gs.at[3], gr.at[3])

    hops(0)
    merge_own.wait()
    wait_bytes(ows.at[1 - core], swap_r.at[2])
    for s in range(2):
        v = ows[s].astype(F32)
        for j in range(2):
            owf[8 * s : 8 * s + 8, 1024 * j : 1024 * j + 1024] = v[8 * j : 8 * j + 8, :]
    owm[...] = owf[...].astype(BF16)
    own_lanes = pl.ds(my_lanes, 1024)
    put = pltpu.make_async_copy(owm.at[:, own_lanes], wo.at[y, xl, z, xh, :, own_lanes], local.at[2])
    put.start()
    hops(1)
    put.wait()
    set_o.begin()
    hops(2)
    hops(3)
    hops(4)

    for q in range(4):
        for s in range(2):
            v = bcs[q, s].astype(F32)
            for j in range(8):
                bcf[4 * q + 2 * s : 4 * q + 2 * s + 2, 256 * j : 256 * j + 256] = v[2 * j : 2 * j + 2, :]
    bcm[...] = bcf[...].astype(BF16)
    put = pltpu.make_async_copy(bcm, wb.at[y, core, xl, xh], local.at[1])
    put.start()
    put.wait()
    set_b.begin()
    set_i.begin()
    set_o.first()
    set_b.first()
    set_i.first()
    set_o.second()
    for j in (0, 1, 3, 2):
        set_o.third(j)
    set_b.second()
    set_i.second()

    tok_own.wait()
    wait_bytes(xs.at[1 - core], swap_r.at[0])
    raw = dot_nt(xs[...].reshape(ROWS, 2048), dtw[...]).astype(BF16)
    row = lax.broadcasted_iota(jnp.int32, (64, 32), 0)
    col = lax.broadcasted_iota(jnp.int32, (64, 32), 1)
    pick = row == head_map(core, (64, 32), 1) + 32 * (col // 16)
    v = dot_nn(raw, pick.astype(BF16))
    dt = jnp.maximum(v, 0.0) + jnp.log1p(jnp.exp(-jnp.abs(v)))
    dts[...] = dt

    set_b.third(0)
    set_i.third(0)
    for j in range(4):
        set_o.fourth(j)
    for part in range(2):
        for way in range(2):
            o_send(z, way, 0, part)
    o_swap(z, 0)

    def choose(ref):
        one = (lax.broadcasted_iota(jnp.int32, (32, 16), 0) == head_map(core, (32, 16), 1)).astype(BF16)
        wide_ref = jnp.broadcast_to(ref[...], (8, 32))
        return sum(dot_nn(p, one) for p in parts3(wide_ref))

    rate = choose(decay)
    skips = widen(choose(skip))
    rates = jnp.concatenate([rate, rate], axis=1)[:1]
    step = -dt * rates
    logdt = jnp.log(dt)
    r = lax.broadcasted_iota(jnp.int32, (BLOCK, BLOCK), 0)
    c = lax.broadcasted_iota(jnp.int32, (BLOCK, BLOCK), 1)
    lower = (c <= r).astype(BF16)
    upper = (c >= r).astype(BF16)
    fwd_col = lax.broadcasted_iota(jnp.int32, (BLOCK, 32), 1) < 16
    for b in range(NBLK):
        rows = slice(b * BLOCK, b * BLOCK + BLOCK)
        sp = parts3(step[rows])
        lam = jnp.where(fwd_col, sum(dot_nn(lower, p) for p in sp), sum(dot_nn(upper, p) for p in sp))
        lams[rows, :] = lam
        padded = jnp.concatenate([lam - logdt[rows], jnp.zeros((BLOCK, 96), F32)], axis=1)
        lamt[b] = jnp.transpose(padded)[:32]

    set_b.third(1)
    set_b.third(3)
    set_i.third(1)
    set_i.third(3)
    set_b.third(2)
    set_i.third(2)
    set_g.begin()
    for j in range(4):
        set_b.fourth(j)
    swaps = [remote(wb.at[:, core], wb.at[:, core], swap_s.at[1], swap_r.at[1], partner)]
    swaps[0].start()

    for d in range(2):
        cols = slice(16 * d, 16 * d + 16)
        for b in range(NBLK):
            rows = slice(b * BLOCK, b * BLOCK + BLOCK)
            lam = lams[rows, cols]
            end = lam[BLOCK - 1 : BLOCK] if d == 0 else lam[0:1]
            wide_f[d, rows, :] = widen(jnp.exp(end - lam) * dts[rows, cols])
            wl = widen(jnp.exp(lam))
            wide_l[d, rows, :] = wl
            dend[d, b] = wl[BLOCK - 1 : BLOCK] if d == 0 else wl[0:1]

    wait_bytes(wb.at[:, 1 - core], swap_r.at[1])
    bco[...] = dot_nt(xs[...].reshape(ROWS, 2048), wb[...].reshape(512, 2048)).astype(BF16)

    def block_weights(b, carry):
        rows = pl.ds(pl.multiple_of(b * BLOCK, BLOCK), BLOCK)
        gf = dot_nt(bco[rows, 128:256], bco[rows, 0:128])
        gb = dot_nt(bco[rows, 384:512], bco[rows, 256:384])
        g = jnp.where(r > c, gf, jnp.where(r < c, gb, 0.0))
        lam = lams[rows, :]
        lt = lamt[b]
        for lh in range(16):
            gap_f = lam[:, lh : lh + 1] - lt[lh : lh + 1, :]
            gap_b = lam[:, 16 + lh : 17 + lh] - lt[16 + lh : 17 + lh, :]
            w = g * jnp.exp(jnp.where(r > c, gap_f, gap_b))
            wm[b, :, 128 * lh : 128 * lh + 128] = w.astype(BF16)
        return carry

    lax.fori_loop(0, NBLK, block_weights, 0)

    for j in range(4):
        set_i.fourth(j)
    o_turn(1)
    for g in range(4):
        w = wz[1, g].reshape(256, 2048)
        inner[:, 256 * g : 256 * g + 256] = dot_nt(xs[...].reshape(ROWS, 2048), w).astype(BF16)

    decay_rows = []
    for d in range(2):
        state = jnp.zeros((BLOCK, WIDE), F32)
        decays = jnp.ones((1, WIDE), F32)
        for b in range(NBLK) if d == 0 else reversed(range(NBLK)):
            rows = slice(b * BLOCK, b * BLOCK + BLOCK)
            scaled = (wide_f[d, rows, :] * inner[rows, :].astype(F32)).astype(BF16)
            k = dot_tn(bco[rows, 256 * d : 256 * d + 128], scaled)
            de = dend[d, b]
            kst[d, b] = k
            state = de * state + k
            decays = decays * de
        for j in range(16):
            q, nh = j // 2, j % 2
            pay[j, 64 * d : 64 * d + 64, :] = state[64 * nh : 64 * nh + 64, 128 * q : 128 * q + 128].astype(BF16)
        decay_rows += list(parts3(decays))
    tail = jnp.concatenate([p.astype(F32) for p in decay_rows] + [jnp.zeros((10, WIDE), F32)], axis=0).astype(BF16)
    for j in range(16):
        q = j // 2
        pay[j, 128:144, :] = tail[:, 128 * q : 128 * q + 128]

    def send_states(src, dst, ss, rs):
        cs = []
        for k in range(1, 16):
            j = (chip + k) % 16
            c = remote(src.at[j], dst.at[chip], ss.at[k - 1], rs.at[k - 1], state_peer(j))
            c.start()
            cs.append(c)
        dst[pl.ds(chip, 1)] = src[pl.ds(chip, 1)]
        return cs

    def wait_states(dst, rs):
        for k in range(1, 16):
            wait_bytes(dst.at[(chip - k) % 16], rs.at[k - 1])

    state_copies = send_states(pay, got, s1, r1)
    set_g.first()
    set_g.second()

    left = lax.broadcasted_iota(jnp.int32, (BLOCK, BLOCK), 1) < 64

    def block_intra(b, carry):
        rows = pl.ds(pl.multiple_of(b * BLOCK, BLOCK), BLOCK)
        for q in range(8):
            pair = inner[rows, 128 * q : 128 * q + 128]
            zero = jnp.zeros_like(pair)
            stack = jnp.concatenate([jnp.where(left, pair, zero), jnp.where(left, zero, pair)], axis=0)
            out = dot_nn(wm[b, :, 256 * q : 256 * q + 256], stack)
            yo[rows, 128 * q : 128 * q + 128] = out + skips[:1, 128 * q : 128 * q + 128] * pair.astype(F32)
        return carry

    lax.fori_loop(0, NBLK, block_intra, 0)

    o_turn(2)
    for j in (0, 1, 3, 2):
        set_g.third(j)
    wait_states(got, r1)
    for d in range(2):
        state = jnp.zeros((64, 128), F32)
        for i in range(16) if d == 0 else reversed(range(16)):
            reply[i, 64 * d : 64 * d + 64, :] = state.astype(BF16)
            ds = got[i, 128:144, :].astype(F32)
            de = ds[3 * d : 3 * d + 1] + ds[3 * d + 1 : 3 * d + 2] + ds[3 * d + 2 : 3 * d + 3]
            state = de * state + got[i, 64 * d : 64 * d + 64, :].astype(F32)
    state_copies += send_states(reply, ent, s2, r2)

    o_turn(3)
    for j in range(4):
        set_g.fourth(j)
    for g in range(4):
        w = wz[0, g].reshape(256, 2048)
        gate = dot_nt(xs[...].reshape(ROWS, 2048), w).astype(BF16).astype(F32)
        wide_f[0, :, 256 * g : 256 * g + 256] = gate / (1.0 + jnp.exp(-gate))
    o_turn(4)
    wait_states(ent, r2)
    for q in range(8):
        cols = slice(128 * q, 128 * q + 128)
        for nh in range(2):
            piece = ent[2 * q + nh].astype(F32)
            enter[0, 64 * nh : 64 * nh + 64, cols] = piece[:64]
            enter[1, 64 * nh : 64 * nh + 64, cols] = piece[64:]
    for d in range(2):
        state = enter[d]
        for b in range(NBLK) if d == 0 else reversed(range(NBLK)):
            rows = slice(b * BLOCK, b * BLOCK + BLOCK)
            cv = bco[rows, 256 * d + 128 : 256 * d + 256]
            yo[rows, :] = yo[rows, :] + wide_l[d, rows, :] * dot_nn(cv, state.astype(BF16))
            state = dend[d, b] * state + kst[d, b]

    theirs = pl.ds(pl.multiple_of((1 - core) * 256, 256), 256)
    mine = pl.ds(pl.multiple_of(core * 256, 256), 256)
    squares = jnp.zeros((ROWS, 1), F32)
    pair_copies = []
    for g in range(4):
        cols = slice(256 * g, 256 * g + 256)
        gated = yo[:, cols] * wide_f[0, :, cols]
        squares = squares + jnp.sum(gated * gated, axis=1, keepdims=True)
        for i in range(2 * g, 2 * g + 2):
            place = pl.ds(natural(core, i), 128)
            cols = slice(128 * i, 128 * i + 128)
            part = gated[:, 128 * (i % 2) : 128 * (i % 2) + 128]
            gbuf[:, cols] = (part * gain[0:1, place]).astype(BF16)
            cp = remote(gbuf.at[theirs, cols], wide.at[:, place], ps.at[i], pr.at[i], partner)
            cp.start()
            pair_copies.append(cp)
            wide[:, place] = gbuf[mine, cols]
    sqb[...] = jnp.broadcast_to(squares, (ROWS, 128))
    cp = remote(sqb.at[theirs], sqf, ps.at[8], pr.at[8], partner)
    cp.start()
    pair_copies.append(cp)

    for i in range(8):
        wait_bytes(wide.at[:, pl.ds(natural(1 - core, i), 128)], pr.at[i])
    wait_bytes(sqf, pr.at[8])
    scale = lax.rsqrt((sqb[mine, :1] + sqf[:, :1]) * (1.0 / 2048.0) + 1e-05)
    far_lanes = pl.multiple_of(1024 * (1 - core), 1024)
    for d in range(8):
        for part in range(2):
            wait_bytes(wo.at[:, :, (z - d) % 8, :, :, pl.ds(far_lanes + 512 * part, 512)], osw_r.at[d, part])
    for g in range(8):
        w = wo[g // 2, g % 2].reshape(256, 2048)
        result[:, 256 * g : 256 * g + 256] = (dot_nt(wide[...], w) * scale).astype(BF16)

    for done in dones:
        done()
    for s in (set_b, set_i, set_g, set_o):
        s.drain()
    tok_far.wait_send()
    merge.wait_send()
    for cp in swaps + state_copies + pair_copies + o_copies:
        cp.wait_send()


ANY = pl.BlockSpec(memory_space=pl.ANY)
INV = pl.BlockSpec(memory_space=pltpu.VMEM)


def layer(zx, bc, ow, tok, dtw, decay, skip, gain):
    dma = pltpu.SemaphoreType.DMA
    vm = pltpu.VMEM
    return pl.pallas_call(
        kernel,
        out_shape=jax.ShapeDtypeStruct((256, 2048), BF16),
        in_specs=[ANY, INV, ANY, ANY, INV, INV, INV, INV],
        out_specs=INV,
        scratch_shapes=[
            vm((2, 4, 2, 2, 2, 32, 2048), BF16), vm((4, 2, 2, 2, 16, 2048), BF16),
            vm((4, 2, 8, 2, 16, 2048), BF16), vm((2, 256, 2048), BF16),
            vm((16, 256), BF16), vm((16, 256), F32),
            vm((4, 2, 16, 256), BF16), vm((2, 16, 1024), BF16),
            vm((16, 2048), BF16), vm((16, 2048), F32), vm((16, 2048), BF16), vm((16, 2048), F32),
            vm((ROWS, WIDE), BF16), vm((ROWS, 512), BF16), vm((ROWS, 32), F32), vm((ROWS, 32), F32),
            vm((NBLK, 32, BLOCK), F32), vm((2, ROWS, WIDE), F32), vm((2, ROWS, WIDE), F32),
            vm((NBLK, BLOCK, 2048), BF16), vm((2, NBLK, BLOCK, WIDE), F32), vm((2, NBLK, 1, WIDE), F32),
            vm((ROWS, WIDE), F32), vm((2, BLOCK, WIDE), F32),
            vm((16, 144, 128), BF16), vm((16, 144, 128), BF16), vm((16, 128, 128), BF16),
            vm((16, 128, 128), BF16), vm((ROWS, WIDE), BF16), vm((256, 2048), BF16),
            vm((ROWS, 128), F32), vm((256, 128), F32),
            dma((2,)), dma((2, 2)), dma((2, 2, 4)), dma((2, 4)), dma((3,)), dma((4, 2, 20)), dma((4, 2, 20)),
            dma((2, 4, 2)), dma((2, 4, 2)), dma((8, 2)), dma((8, 2)), dma((3,)), dma((3,)),
            dma((15,)), dma((15,)), dma((15,)), dma((15,)), dma((9,)), dma((9,)),
        ],
        compiler_params=pltpu.CompilerParams(
            collective_id=0, has_side_effects=True, vmem_limit_bytes=VMEM_BYTES
        ),
        name="layer",
    )(zx, bc, ow, tok, dtw, decay, skip, gain)


def shards(tokens, zx_weight, bc_weight, dt_weight, decay_rate, skip_gain, norm_gain, out_weight):
    ow = out_weight.T.reshape(8, 2, 1024).transpose(1, 0, 2).reshape(16, 1024)
    return layer(
        zx_weight.T, bc_weight.T, ow, tokens[0], dt_weight.T,
        decay_rate[None], skip_gain[None], norm_gain[None],
    )[None]


def solution(mesh):
    columns = P(None, ("fsdp", "ctx"))
    in_specs = (P("fsdp", "ctx", None), columns, columns, P(), P(), P(), P(), columns)
    return jax.shard_map(
        shards, mesh=mesh, in_specs=in_specs, out_specs=P("fsdp", "ctx", None), check_vma=False
    )
```

```python
import functools

import jax
import jax.numpy as jnp
from jax import lax
from jax.experimental import pallas as pl
from jax.experimental.pallas import tpu as pltpu
from jax.sharding import PartitionSpec as P

MESH = pl.DeviceIdType.MESH
F32 = jnp.float32
BF16 = jnp.bfloat16
BLOCK = 128
ROWS = 512
NBLK = ROWS // BLOCK
WIDE = 1024
VMEM_BYTES = 60 * 1024 * 1024


def coords():
    f = lax.axis_index("fsdp")
    c = lax.axis_index("ctx")
    y, xl = f // 2, f % 2
    z, xh, core = c // 4, (c // 2) % 2, c % 2
    return y, xl, z, xh, core


def dev(y, x, z, core):
    return (y * 2 + x % 2, z * 4 + (x // 2) * 2 + core)


def dot_nt(a, b):
    return lax.dot_general(a, b, (((1,), (1,)), ((), ())), preferred_element_type=F32)


def dot_tn(a, b):
    return lax.dot_general(a, b, (((0,), (0,)), ((), ())), preferred_element_type=F32)


def dot_nn(a, b):
    return lax.dot_general(a, b, (((1,), (0,)), ((), ())), preferred_element_type=F32)


def parts3(v):
    hi = v.astype(BF16)
    r = v - hi.astype(F32)
    mid = r.astype(BF16)
    lo = (r - mid.astype(F32)).astype(BF16)
    return hi, mid, lo


def wait_bytes(ref, sem):
    pltpu.make_async_copy(ref, ref, sem).wait()


class Ring:
    def __init__(self, view, slot, send, recv):
        self.view, self.slot, self.send, self.recv = view, slot, send, recv
        self.started = []

    def ref(self, half, j, m, part=None):
        y, xl, z, xh, core = coords()
        x = xh * 2 + xl
        dy, dx = (j, m) if half == 0 else (m, j)
        return self.view(half, self.slot((y - dy) % 4), (x - dx) % 4, part)

    def copy(self, half, ref, axis, step, index):
        y, xl, z, xh, core = coords()
        x = xh * 2 + xl
        to = dev((y + step) % 4, x, z, core) if axis == half else dev(y, (x + step) % 4, z, core)
        c = pltpu.make_async_remote_copy(
            src_ref=ref, dst_ref=ref, send_sem=self.send.at[half, index], recv_sem=self.recv.at[half, index],
            device_id=to, device_id_type=MESH,
        )
        c.start()
        self.started.append(c)

    def wait(self, half, ref, index):
        wait_bytes(ref, self.recv.at[half, index])

    def both(self, half, j):
        ref = self.ref(half, j, 0)
        self.copy(half, ref, 1, 1, 4 + 4 * j)
        self.copy(half, ref, 1, 3, 5 + 4 * j)

    def begin(self):
        for half in range(2):
            ref = self.ref(half, 0, 0)
            self.copy(half, ref, 0, 1, 0)
            self.copy(half, ref, 0, 3, 1)
        for half in range(2):
            self.both(half, 0)

    def turn(self, half, axis, base, block):
        self.wait(half, block(1), base)
        self.copy(half, block(1, 0), axis, 1, base + 2)
        self.wait(half, block(3), base + 1)
        self.copy(half, block(3, 1), axis, 3, base + 3)

    def first(self):
        for half in range(2):
            self.turn(half, 0, 0, lambda n, part=None: self.ref(half, n, 0, part))
        for half in range(2):
            self.both(half, 1)
            self.both(half, 3)

    def second(self):
        for half in range(2):
            for part in range(2):
                self.wait(half, self.ref(half, 2, 0, part), 2 + part)
            self.both(half, 2)

    def third(self, j):
        for half in range(2):
            self.turn(half, 1, 4 + 4 * j, lambda n, part=None: self.ref(half, j, n, part))

    def fourth(self, j):
        for half in range(2):
            for part in range(2):
                self.wait(half, self.ref(half, j, 2, part), 6 + 4 * j + part)

    def drain(self):
        for c in self.started:
            c.wait_send()


def head_map(lane, shape, axis):
    i = lax.broadcasted_iota(jnp.int32, shape, axis)
    zl, xl, yy, t = i % 2, (i // 2) % 2, (i // 4) % 2, (i // 8) % 2
    return (yy * 2 + xl) * 8 + lane * 4 + t * 2 + zl


def natural(lane, g):
    y, xl = g // 2, g % 2
    yy, t = y % 2, y // 2
    return pl.multiple_of(((yy * 2 + xl) * 8 + lane * 4 + t * 2) * 64, 128)


def widen(v):
    stacked = jnp.concatenate(parts3(v), axis=1)
    r = lax.broadcasted_iota(jnp.int32, (48, WIDE), 0)
    c = lax.broadcasted_iota(jnp.int32, (48, WIDE), 1)
    spread = (r % 16 == c // 64).astype(BF16)
    return dot_nn(stacked, spread)


def kernel(
    zx, bc, ow, tok, dtw, decay, skip, gain, result,
    wz, wb, wo, xs, bst, bstf, bcs, ows, bcm, bcf, owm, owf,
    inner, bco, lams, dts, lamt, wide_f, wide_l, wm, kst, dend, yo, enter,
    pay_f, pay_b, got_f, got_b, reply, ent, gbuf, wide, sqb, sqf,
    zsend, zrecv, bsend, brecv, local, gs, gr, ozs, ozr, osw_s, osw_r, o2s, o2r,
    swap_s, swap_r, s1, r1, s2, r2, ps, pr,
):
    y, xl, z, xh, core = coords()
    x = xh * 2 + xl
    h, zc = z // 4, z % 4
    t, zl = zc // 2, zc % 2
    inner_side, yy = y // 2, y % 2
    ys = yy + 2 * t
    y_to = yy + 2 * ((t + 1 + inner_side) % 2)
    chip = z * 2 + xh
    partner = dev(y, x, z, 1 - core)

    def state_peer(j):
        return dev(y, (j % 2) * 2 + xl, j // 2, core)

    def remote(src, dst, ss, rs, to):
        return pltpu.make_async_remote_copy(
            src_ref=src, dst_ref=dst, send_sem=ss, recv_sem=rs, device_id=to, device_id_type=MESH
        )

    barrier = pltpu.get_barrier_semaphore()
    peers = []
    for dz in range(8):
        for dc in range(2):
            for dy in (0, 2):
                if (dz, dc, dy) != (0, 0, 0):
                    peers.append(dev((y + dy) % 4, x, (z + dz) % 8, (core + dc) % 2))
        peers.append(dev(y, (x + 2) % 4, (z + dz) % 8, core))
    for k in (1, 3):
        peers.append(dev((y + k) % 4, x, z, core))
        peers.append(dev(y, (x + k) % 4, z, core))
    for to in peers:
        pl.semaphore_signal(barrier, inc=1, device_id=to, device_id_type=MESH)
    for j in range(8):
        bstf[2 * j : 2 * j + 2, :] = bc[:, 256 * j : 256 * j + 256].astype(F32)
    bst[...] = bstf[...].astype(BF16)
    pl.semaphore_wait(barrier, len(peers))

    def own_z(g, sy, sl, src_core):
        return wz.at[g, sy, xl, sl, xh, pl.ds(src_core * 16, 16)]

    def first(src, dst, to_y, send, recv):
        is_self = jnp.logical_and(to_y == y, h == core)
        for dz in (0, 1, 7, 2, 6, 3, 5, 4):
            c = remote(src, dst, send.at[dz], recv, dev(to_y, x, (z + dz) % 8, h))
            if dz:
                c.start()
            else:

                @pl.when(is_self)
                def _():
                    pltpu.make_async_copy(src, dst, recv).start()

                @pl.when(jnp.logical_not(is_self))
                def _():
                    c.start()

        def done():
            for dz in range(8):
                if dz:
                    wait_bytes(src, send.at[dz])
                else:

                    @pl.when(jnp.logical_not(is_self))
                    def _():
                        wait_bytes(src, send.at[0])

        return done

    dones = [
        first(bst, bcs.at[zc, core], y, bsend, brecv.at[zc, core]),
        first(zx, own_z(inner_side, ys, zl, core), y_to, zsend, zrecv.at[inner_side, zl, core]),
    ]
    merge = remote(ow, ows.at[core], swap_s.at[2], swap_r.at[2], partner)
    merge.start()
    merge_own = pltpu.make_async_copy(ow, ows.at[core], local.at[2])
    merge_own.start()
    tok_own = pltpu.make_async_copy(tok, xs.at[core], local.at[0])
    tok_own.start()
    tok_far = remote(tok, xs.at[core], swap_s.at[0], swap_r.at[0], partner)
    tok_far.start()

    def view_b(half, sy, sx, part):
        lanes = pl.ds(1024 * half, 1024) if part is None else pl.ds(1024 * half + 512 * part, 512)
        return wb.at[sy, core, sx % 2, sx // 2, :, lanes]

    def view_g(g):
        def view(half, sy, sx, part):
            rows = pl.ds(0, 32) if part is None else pl.ds(16 * part, 16)
            return wz.at[g, sy, sx % 2, half, sx // 2, rows]

        return view

    my_lanes = pl.multiple_of(1024 * core, 1024)

    my_lanes = pl.multiple_of(1024 * core, 1024)
    far_lanes = pl.multiple_of(1024 * (1 - core), 1024)

    def view_o1(half, sy, sx, part):
        lanes = pl.ds(my_lanes + 256 * half, 256) if part is None else pl.ds(my_lanes + 256 * half + 128 * part, 128)
        return wo.at[sy, sx % 2, z, sx // 2, :, lanes]

    def view_o2(half, sy, sx, part):
        zs = pl.ds(4 * half, 4) if part is None else pl.ds(4 * half + 2 * part, 2)
        return wo.at[sy, sx % 2, zs, sx // 2, :, pl.ds(my_lanes + 512, 512)]

    def plane(zsrc, part, base=None):
        return wo.at[:, :, zsrc, :, :, pl.ds((my_lanes if base is None else base) + 256 * part, 256)]

    def corner(half, j, base):
        lanes = pl.ds(base + 512, 512)
        if half == 0:
            return wo.at[(y - j) % 4, :, pl.ds(0, 4), :, :, lanes]
        sx = (x - j) % 4
        return wo.at[:, sx % 2, pl.ds(4, 4), sx // 2, :, lanes]

    o_copies = []

    def o_send(zsrc, way, d, part):
        ref = plane(zsrc, part)
        to = dev(y, x, (z + 1 + 6 * way) % 8, core)
        cp = remote(ref, ref, ozs.at[way, d, part], ozr.at[way, d, part], to)
        cp.start()
        o_copies.append(cp)

    def o_hand(ref, index):
        cp = remote(ref, ref, osw_s.at[index], osw_r.at[index], partner)
        cp.start()
        o_copies.append(cp)

    def o_swap(zsrc, d):
        for part in range(2):
            o_hand(plane(zsrc, part), 2 * d + part)

    def o_turn(d):
        for way in range(2):
            zsrc = (z - d) % 8 if way == 0 else (z + d) % 8
            for part in range(2):
                if d < 4 or part == way:
                    wait_bytes(plane(zsrc, part), ozr.at[way, d - 1, part])
                if d < 3 or (d == 3 and part == way):
                    o_send(zsrc, way, d, part)
        for way in range(2):
            zsrc = (z - d) % 8 if way == 0 else (z + d) % 8
            if d < 4 or way == 0:
                o_swap(zsrc, d if way == 0 else 8 - d)

    same = lambda v: v
    flip = lambda v: (v + 2) % 4
    set_b = Ring(view_b, same, gs.at[0], gr.at[0])
    set_i = Ring(view_g(1), same, gs.at[1], gr.at[1])
    set_g = Ring(view_g(0), flip, gs.at[2], gr.at[2])
    set_o = Ring(view_o1, same, gs.at[3], gr.at[3])
    set_p = Ring(view_o2, same, gs.at[4], gr.at[4])

    merge_own.wait()
    wait_bytes(ows.at[1 - core], swap_r.at[2])
    for s in range(2):
        v = ows[s].astype(F32)
        for j in range(2):
            owf[8 * s : 8 * s + 8, 1024 * j : 1024 * j + 1024] = v[8 * j : 8 * j + 8, :]
    owm[...] = owf[...].astype(BF16)
    own_lanes = pl.ds(my_lanes, 1024)
    put = pltpu.make_async_copy(owm.at[:, own_lanes], wo.at[y, xl, z, xh, :, own_lanes], local.at[2])
    put.start()
    put.wait()
    set_o.begin()

    tok_own.wait()
    wait_bytes(xs.at[1 - core], swap_r.at[0])
    raw = dot_nt(xs[...].reshape(ROWS, 2048), dtw[...]).astype(BF16)
    row = lax.broadcasted_iota(jnp.int32, (64, 32), 0)
    col = lax.broadcasted_iota(jnp.int32, (64, 32), 1)
    pick = row == head_map(core, (64, 32), 1) + 32 * (col // 16)
    v = dot_nn(raw, pick.astype(BF16))
    dt = jnp.maximum(v, 0.0) + jnp.log1p(jnp.exp(-jnp.abs(v)))
    dts[...] = dt

    def choose(ref):
        one = (lax.broadcasted_iota(jnp.int32, (32, 16), 0) == head_map(core, (32, 16), 1)).astype(BF16)
        wide_ref = jnp.broadcast_to(ref[...], (8, 32))
        return sum(dot_nn(p, one) for p in parts3(wide_ref))

    rate = choose(decay)
    skips = widen(choose(skip))
    rates = jnp.concatenate([rate, rate], axis=1)[:1]
    step = -dt * rates
    logdt = jnp.log(dt)
    r = lax.broadcasted_iota(jnp.int32, (BLOCK, BLOCK), 0)
    c = lax.broadcasted_iota(jnp.int32, (BLOCK, BLOCK), 1)
    lower = (c <= r).astype(BF16)
    upper = (c >= r).astype(BF16)
    fwd_col = lax.broadcasted_iota(jnp.int32, (BLOCK, 32), 1) < 16
    for b in range(NBLK):
        rows = slice(b * BLOCK, b * BLOCK + BLOCK)
        sp = parts3(step[rows])
        lam = jnp.where(fwd_col, sum(dot_nn(lower, p) for p in sp), sum(dot_nn(upper, p) for p in sp))
        lams[rows, :] = lam
        padded = jnp.concatenate([lam - logdt[rows], jnp.zeros((BLOCK, 96), F32)], axis=1)
        lamt[b] = jnp.transpose(padded)[:32]

    for d in range(2):
        cols = slice(16 * d, 16 * d + 16)
        for b in range(NBLK):
            rows = slice(b * BLOCK, b * BLOCK + BLOCK)
            lam = lams[rows, cols]
            end = lam[BLOCK - 1 : BLOCK] if d == 0 else lam[0:1]
            wide_f[d, rows, :] = widen(jnp.exp(end - lam) * dts[rows, cols])
            wl = widen(jnp.exp(lam))
            wide_l[d, rows, :] = wl
            dend[d, b] = wl[BLOCK - 1 : BLOCK] if d == 0 else wl[0:1]


    set_o.first()
    set_o.second()
    for j in (0, 1, 3, 2):
        set_o.third(j)

    for q in range(4):
        for s in range(2):
            wait_bytes(bcs.at[q, s], brecv.at[q, s])
    for q in range(4):
        for s in range(2):
            v = bcs[q, s].astype(F32)
            for j in range(8):
                bcf[4 * q + 2 * s : 4 * q + 2 * s + 2, 256 * j : 256 * j + 256] = v[2 * j : 2 * j + 2, :]
    bcm[...] = bcf[...].astype(BF16)
    put = pltpu.make_async_copy(bcm, wb.at[y, core, xl, xh], local.at[1])
    put.start()
    put.wait()
    set_b.begin()
    for s in range(2):
        for q in range(2):
            wait_bytes(own_z(1, y, s, q), zrecv.at[1, s, q])
    set_i.begin()
    for j in range(4):
        set_o.fourth(j)
    for part in range(2):
        for way in range(2):
            o_send(z, way, 0, part)
    o_swap(z, 0)
    set_b.first()
    set_i.first()
    for k in (1, 7, 2, 6, 3, 5, 4):
        ref = wo.at[y, xl, z, xh, :, pl.ds(my_lanes + 512, 512)]
        cp = remote(ref, ref, o2s.at[k - 1], o2r.at[k - 1], dev(y, x, (z + k) % 8, core))
        cp.start()
        o_copies.append(cp)
    set_b.second()
    set_i.second()
    for j in (0, 1, 3, 2):
        set_b.third(j)
        set_i.third(j)
        if j == 1:
            o_turn(1)
    for j in range(4):
        set_b.fourth(j)
    swaps = [remote(wb.at[:, core], wb.at[:, core], swap_s.at[1], swap_r.at[1], partner)]
    swaps[0].start()
    o_turn(2)
    wait_bytes(wb.at[:, 1 - core], swap_r.at[1])
    bco[...] = dot_nt(xs[...].reshape(ROWS, 2048), wb[...].reshape(512, 2048)).astype(BF16)

    def block_weights(b, carry):
        rows = pl.ds(pl.multiple_of(b * BLOCK, BLOCK), BLOCK)
        gf = dot_nt(bco[rows, 128:256], bco[rows, 0:128])
        gb = dot_nt(bco[rows, 384:512], bco[rows, 256:384])
        g = jnp.where(r > c, gf, jnp.where(r < c, gb, 0.0))
        lam = lams[rows, :]
        lt = lamt[b]
        for lh in range(16):
            gap_f = lam[:, lh : lh + 1] - lt[lh : lh + 1, :]
            gap_b = lam[:, 16 + lh : 17 + lh] - lt[16 + lh : 17 + lh, :]
            w = g * jnp.exp(jnp.where(r > c, gap_f, gap_b))
            wm[b, :, 128 * lh : 128 * lh + 128] = w.astype(BF16)
        return carry

    lax.fori_loop(0, NBLK, block_weights, 0)

    for j in range(4):
        set_i.fourth(j)
    for s in range(2):
        for q in range(2):
            wait_bytes(own_z(0, flip(y), s, q), zrecv.at[0, s, q])
    set_g.begin()
    for k in range(1, 8):
        wait_bytes(wo.at[y, xl, (z - k) % 8, xh, :, pl.ds(my_lanes + 512, 512)], o2r.at[k - 1])
    set_p.begin()
    for g in range(4):
        w = wz[1, g].reshape(256, 2048)
        inner[:, 256 * g : 256 * g + 256] = dot_nt(xs[...].reshape(ROWS, 2048), w).astype(BF16)

    def send_states(src, dst, ss, rs):
        cs = []
        for k in (8, 7, 9, 6, 10, 5, 11, 4, 12, 3, 13, 2, 14, 1, 15):
            j = (chip + k) % 16
            c = remote(src.at[j], dst.at[chip], ss.at[k - 1], rs.at[k - 1], state_peer(j))
            c.start()
            cs.append(c)
        dst[pl.ds(chip, 1)] = src[pl.ds(chip, 1)]
        return cs

    def wait_states(dst, rs):
        for k in range(1, 16):
            wait_bytes(dst.at[(chip - k) % 16], rs.at[k - 1])

    both_decays = []
    for d in range(2):
        decays = dend[d, 0]
        for b in range(1, NBLK):
            decays = decays * dend[d, b]
        both_decays += [p.astype(F32) for p in parts3(decays)]
    tail = jnp.concatenate(both_decays + [jnp.zeros((10, WIDE), F32)], axis=0).astype(BF16)
    state_copies = []
    for d in range(2):
        pay = (pay_f, pay_b)[d]
        state = jnp.zeros((BLOCK, WIDE), F32)
        for b in range(NBLK) if d == 0 else reversed(range(NBLK)):
            rows = slice(b * BLOCK, b * BLOCK + BLOCK)
            scaled = (wide_f[d, rows, :] * inner[rows, :].astype(F32)).astype(BF16)
            k = dot_tn(bco[rows, 256 * d : 256 * d + 128], scaled)
            kst[d, b] = k
            state = dend[d, b] * state + k
        for j in range(16):
            q, nh = j // 2, j % 2
            pay[j, :64, :] = state[64 * nh : 64 * nh + 64, 128 * q : 128 * q + 128].astype(BF16)
            if d == 0:
                pay[j, 64:80, :] = tail[:, 128 * q : 128 * q + 128]
        state_copies += send_states(pay, (got_f, got_b)[d], s1.at[d], r1.at[d])
    o_turn(3)
    set_g.first()
    set_g.second()

    left = lax.broadcasted_iota(jnp.int32, (BLOCK, BLOCK), 1) < 64

    def block_intra(b, carry):
        rows = pl.ds(pl.multiple_of(b * BLOCK, BLOCK), BLOCK)
        for q in range(8):
            pair = inner[rows, 128 * q : 128 * q + 128]
            zero = jnp.zeros_like(pair)
            stack = jnp.concatenate([jnp.where(left, pair, zero), jnp.where(left, zero, pair)], axis=0)
            out = dot_nn(wm[b, :, 256 * q : 256 * q + 256], stack)
            yo[rows, 128 * q : 128 * q + 128] = out + skips[:1, 128 * q : 128 * q + 128] * pair.astype(F32)
        return carry

    lax.fori_loop(0, NBLK, block_intra, 0)

    for d in range(2):
        got = (got_f, got_b)[d]
        wait_states(got, r1.at[d])
        state = jnp.zeros((64, 128), F32)
        for i in range(16) if d == 0 else reversed(range(16)):
            reply[d, i] = state.astype(BF16)
            ds = got_f[i, 64:80, :].astype(F32)
            de = ds[3 * d : 3 * d + 1] + ds[3 * d + 1 : 3 * d + 2] + ds[3 * d + 2 : 3 * d + 3]
            state = de * state + got[i, :64, :].astype(F32)
        state_copies += send_states(reply.at[d], ent.at[d], s2.at[d], r2.at[d])
        if d == 0:
            set_p.first()
            set_p.second()
    for j in (0, 1, 3, 2):
        set_g.third(j)
    o_turn(4)
    for j in (0, 1, 3, 2):
        set_p.third(j)
    for j in range(4):
        set_g.fourth(j)
    for g in range(4):
        w = wz[0, g].reshape(256, 2048)
        gate = dot_nt(xs[...].reshape(ROWS, 2048), w).astype(BF16).astype(F32)
        wide_f[0, :, 256 * g : 256 * g + 256] = gate / (1.0 + jnp.exp(-gate))
    for d in range(2):
        wait_states(ent.at[d], r2.at[d])
        for q in range(8):
            cols = slice(128 * q, 128 * q + 128)
            for nh in range(2):
                enter[64 * nh : 64 * nh + 64, cols] = ent[d, 2 * q + nh].astype(F32)
        state = enter[...]
        for b in range(NBLK) if d == 0 else reversed(range(NBLK)):
            rows = slice(b * BLOCK, b * BLOCK + BLOCK)
            cv = bco[rows, 256 * d + 128 : 256 * d + 256]
            yo[rows, :] = yo[rows, :] + wide_l[d, rows, :] * dot_nn(cv, state.astype(BF16))
            state = dend[d, b] * state + kst[d, b]

    theirs = pl.ds(pl.multiple_of((1 - core) * 256, 256), 256)
    mine = pl.ds(pl.multiple_of(core * 256, 256), 256)
    squares = jnp.zeros((ROWS, 1), F32)
    pair_copies = []
    for g in range(4):
        cols = slice(256 * g, 256 * g + 256)
        gated = yo[:, cols] * wide_f[0, :, cols]
        squares = squares + jnp.sum(gated * gated, axis=1, keepdims=True)
        for i in range(2 * g, 2 * g + 2):
            place = pl.ds(natural(core, i), 128)
            cols = slice(128 * i, 128 * i + 128)
            part = gated[:, 128 * (i % 2) : 128 * (i % 2) + 128]
            gbuf[:, cols] = (part * gain[0:1, place]).astype(BF16)
            cp = remote(gbuf.at[theirs, cols], wide.at[:, place], ps.at[i], pr.at[i], partner)
            cp.start()
            pair_copies.append(cp)
            wide[:, place] = gbuf[mine, cols]
    sqb[...] = jnp.broadcast_to(squares, (ROWS, 128))
    cp = remote(sqb.at[theirs], sqf, ps.at[8], pr.at[8], partner)
    cp.start()
    pair_copies.append(cp)

    for j in (0, 1, 3, 2):
        set_p.fourth(j)
        for half in range(2):
            o_hand(corner(half, j, my_lanes), 16 + 2 * j + half)
    for i in range(8):
        wait_bytes(wide.at[:, pl.ds(natural(1 - core, i), 128)], pr.at[i])
    wait_bytes(sqf, pr.at[8])
    scale = lax.rsqrt((sqb[mine, :1] + sqf[:, :1]) * (1.0 / 2048.0) + 1e-05)
    for d in range(8):
        for part in range(2):
            wait_bytes(plane((z - d) % 8, part, far_lanes), osw_r.at[2 * d + part])
    for j in range(4):
        for half in range(2):
            wait_bytes(corner(half, j, far_lanes), osw_r.at[16 + 2 * j + half])
    for g in range(8):
        w = wo[g // 2, g % 2].reshape(256, 2048)
        result[:, 256 * g : 256 * g + 256] = (dot_nt(wide[...], w) * scale).astype(BF16)

    for done in dones:
        done()
    for s in (set_b, set_i, set_g, set_o, set_p):
        s.drain()
    tok_far.wait_send()
    merge.wait_send()
    for cp in swaps + state_copies + pair_copies + o_copies:
        cp.wait_send()


ANY = pl.BlockSpec(memory_space=pl.ANY)
INV = pl.BlockSpec(memory_space=pltpu.VMEM)


def layer(zx, bc, ow, tok, dtw, decay, skip, gain):
    dma = pltpu.SemaphoreType.DMA
    vm = pltpu.VMEM
    return pl.pallas_call(
        kernel,
        out_shape=jax.ShapeDtypeStruct((256, 2048), BF16),
        in_specs=[ANY, INV, ANY, ANY, INV, INV, INV, INV],
        out_specs=INV,
        scratch_shapes=[
            vm((2, 4, 2, 2, 2, 32, 2048), BF16), vm((4, 2, 2, 2, 16, 2048), BF16),
            vm((4, 2, 8, 2, 16, 2048), BF16), vm((2, 256, 2048), BF16),
            vm((16, 256), BF16), vm((16, 256), F32),
            vm((4, 2, 16, 256), BF16), vm((2, 16, 1024), BF16),
            vm((16, 2048), BF16), vm((16, 2048), F32), vm((16, 2048), BF16), vm((16, 2048), F32),
            vm((ROWS, WIDE), BF16), vm((ROWS, 512), BF16), vm((ROWS, 32), F32), vm((ROWS, 32), F32),
            vm((NBLK, 32, BLOCK), F32), vm((2, ROWS, WIDE), F32), vm((2, ROWS, WIDE), F32),
            vm((NBLK, BLOCK, 2048), BF16), vm((2, NBLK, BLOCK, WIDE), F32), vm((2, NBLK, 1, WIDE), F32),
            vm((ROWS, WIDE), F32), vm((BLOCK, WIDE), F32),
            vm((16, 80, 128), BF16), vm((16, 64, 128), BF16), vm((16, 80, 128), BF16), vm((16, 64, 128), BF16),
            vm((2, 16, 64, 128), BF16), vm((2, 16, 64, 128), BF16), vm((ROWS, WIDE), BF16), vm((256, 2048), BF16),
            vm((ROWS, 128), F32), vm((256, 128), F32),
            dma((8,)), dma((2, 2, 2)), dma((8,)), dma((4, 2)), dma((3,)), dma((5, 2, 20)), dma((5, 2, 20)),
            dma((2, 4, 2)), dma((2, 4, 2)), dma((24,)), dma((24,)), dma((7,)), dma((7,)), dma((3,)), dma((3,)),
            dma((2, 15)), dma((2, 15)), dma((2, 15)), dma((2, 15)), dma((9,)), dma((9,)),
        ],
        compiler_params=pltpu.CompilerParams(
            collective_id=0, has_side_effects=True, vmem_limit_bytes=VMEM_BYTES
        ),
        name="layer",
    )(zx, bc, ow, tok, dtw, decay, skip, gain)


def shards(tokens, zx_weight, bc_weight, dt_weight, decay_rate, skip_gain, norm_gain, out_weight):
    ow = out_weight.T.reshape(8, 2, 1024).transpose(1, 0, 2).reshape(16, 1024)
    return layer(
        zx_weight.T, bc_weight.T, ow, tokens[0], dt_weight.T,
        decay_rate[None], skip_gain[None], norm_gain[None],
    )[None]


def solution(mesh):
    columns = P(None, ("fsdp", "ctx"))
    in_specs = (P("fsdp", "ctx", None), columns, columns, P(), P(), P(), P(), columns)
    return jax.shard_map(
        shards, mesh=mesh, in_specs=in_specs, out_specs=P("fsdp", "ctx", None), check_vma=False
    )
```

```python
import functools

import jax
import jax.numpy as jnp
from jax import lax
from jax.experimental import pallas as pl
from jax.experimental.pallas import tpu as pltpu
from jax.sharding import PartitionSpec as P

MESH = pl.DeviceIdType.MESH
F32 = jnp.float32
BF16 = jnp.bfloat16
BLOCK = 128
PLANE_FIRST = 768
ROWS = 512
NBLK = ROWS // BLOCK
WIDE = 1024
VMEM_BYTES = 60 * 1024 * 1024


def coords():
    f = lax.axis_index("fsdp")
    c = lax.axis_index("ctx")
    y, xl = f // 2, f % 2
    z, xh, core = c // 4, (c // 2) % 2, c % 2
    return y, xl, z, xh, core


def dev(y, x, z, core):
    return (y * 2 + x % 2, z * 4 + (x // 2) * 2 + core)


def dot_nt(a, b):
    return lax.dot_general(a, b, (((1,), (1,)), ((), ())), preferred_element_type=F32)


def dot_tn(a, b):
    return lax.dot_general(a, b, (((0,), (0,)), ((), ())), preferred_element_type=F32)


def dot_nn(a, b):
    return lax.dot_general(a, b, (((1,), (0,)), ((), ())), preferred_element_type=F32)


def parts3(v):
    hi = v.astype(BF16)
    r = v - hi.astype(F32)
    mid = r.astype(BF16)
    lo = (r - mid.astype(F32)).astype(BF16)
    return hi, mid, lo


def wait_bytes(ref, sem):
    pltpu.make_async_copy(ref, ref, sem).wait()


class Ring:
    def __init__(self, view, slot, send, recv, halves=(0, 1)):
        self.view, self.slot, self.send, self.recv, self.halves = view, slot, send, recv, halves
        self.started = []

    def ref(self, half, j, m, part=None):
        y, xl, z, xh, core = coords()
        x = xh * 2 + xl
        dy, dx = (j, m) if half == 0 else (m, j)
        return self.view(half, self.slot((y - dy) % 4), (x - dx) % 4, part)

    def copy(self, half, ref, axis, step, index):
        y, xl, z, xh, core = coords()
        x = xh * 2 + xl
        to = dev((y + step) % 4, x, z, core) if axis == half else dev(y, (x + step) % 4, z, core)
        c = pltpu.make_async_remote_copy(
            src_ref=ref, dst_ref=ref, send_sem=self.send.at[half, index], recv_sem=self.recv.at[half, index],
            device_id=to, device_id_type=MESH,
        )
        c.start()
        self.started.append(c)

    def wait(self, half, ref, index):
        wait_bytes(ref, self.recv.at[half, index])

    def both(self, half, j):
        ref = self.ref(half, j, 0)
        self.copy(half, ref, 1, 1, 4 + 4 * j)
        self.copy(half, ref, 1, 3, 5 + 4 * j)

    def begin(self):
        for half in self.halves:
            ref = self.ref(half, 0, 0)
            self.copy(half, ref, 0, 1, 0)
            self.copy(half, ref, 0, 3, 1)
        for half in self.halves:
            self.both(half, 0)

    def turn(self, half, axis, base, block):
        self.wait(half, block(1), base)
        self.copy(half, block(1, 0), axis, 1, base + 2)
        self.wait(half, block(3), base + 1)
        self.copy(half, block(3, 1), axis, 3, base + 3)

    def first(self):
        for half in self.halves:
            self.turn(half, 0, 0, lambda n, part=None: self.ref(half, n, 0, part))
        for half in self.halves:
            self.both(half, 1)
            self.both(half, 3)

    def second(self):
        for half in self.halves:
            for part in range(2):
                self.wait(half, self.ref(half, 2, 0, part), 2 + part)
            self.both(half, 2)

    def third(self, j):
        for half in self.halves:
            self.turn(half, 1, 4 + 4 * j, lambda n, part=None: self.ref(half, j, n, part))

    def fourth(self, j):
        for half in self.halves:
            for part in range(2):
                self.wait(half, self.ref(half, j, 2, part), 6 + 4 * j + part)

    def drain(self):
        for c in self.started:
            c.wait_send()


def head_map(lane, shape, axis):
    i = lax.broadcasted_iota(jnp.int32, shape, axis)
    zl, xl, yy, t = i % 2, (i // 2) % 2, (i // 4) % 2, (i // 8) % 2
    return (yy * 2 + xl) * 8 + lane * 4 + t * 2 + zl


def natural(lane, g):
    y, xl = g // 2, g % 2
    yy, t = y % 2, y // 2
    return pl.multiple_of(((yy * 2 + xl) * 8 + lane * 4 + t * 2) * 64, 128)


def widen(v):
    stacked = jnp.concatenate(parts3(v), axis=1)
    r = lax.broadcasted_iota(jnp.int32, (48, WIDE), 0)
    c = lax.broadcasted_iota(jnp.int32, (48, WIDE), 1)
    spread = (r % 16 == c // 64).astype(BF16)
    return dot_nn(stacked, spread)


def kernel(
    zx, bc, ow, tok, dtw, decay, skip, gain, result,
    wz, wb, wo, xs, bst, bstf, bcs, ows, bcm, bcf, owm, owf,
    inner, bco, lams, dts, lamt, wide_f, wide_l, wm, kst, dend, yo, enter,
    pay_f, pay_b, got_f, got_b, reply, ent, gbuf, wide, sqb, sqf,
    zsend, zrecv, bsend, brecv, local, gs, gr, ozs, ozr, osw_s, osw_r, o2s, o2r,
    swap_s, swap_r, s1, r1, s2, r2, ps, pr,
):
    y, xl, z, xh, core = coords()
    x = xh * 2 + xl
    h, zc = z // 4, z % 4
    t, zl = zc // 2, zc % 2
    inner_side, yy = y // 2, y % 2
    ys = yy + 2 * t
    y_to = yy + 2 * ((t + 1 + inner_side) % 2)
    chip = z * 2 + xh
    partner = dev(y, x, z, 1 - core)

    def state_peer(j):
        return dev(y, (j % 2) * 2 + xl, j // 2, core)

    def remote(src, dst, ss, rs, to):
        return pltpu.make_async_remote_copy(
            src_ref=src, dst_ref=dst, send_sem=ss, recv_sem=rs, device_id=to, device_id_type=MESH
        )

    barrier = pltpu.get_barrier_semaphore()
    peers = []
    for dz in range(8):
        for dc in range(2):
            for dy in (0, 2):
                if (dz, dc, dy) != (0, 0, 0):
                    peers.append(dev((y + dy) % 4, x, (z + dz) % 8, (core + dc) % 2))
        peers.append(dev(y, (x + 2) % 4, (z + dz) % 8, core))
    for k in (1, 3):
        peers.append(dev((y + k) % 4, x, z, core))
        peers.append(dev(y, (x + k) % 4, z, core))
    for to in peers:
        pl.semaphore_signal(barrier, inc=1, device_id=to, device_id_type=MESH)
    for j in range(8):
        bstf[2 * j : 2 * j + 2, :] = bc[:, 256 * j : 256 * j + 256].astype(F32)
    bst[...] = bstf[...].astype(BF16)
    pl.semaphore_wait(barrier, len(peers))

    def own_z(g, sy, sl, src_core):
        return wz.at[g, sy, xl, sl, xh, pl.ds(src_core * 16, 16)]

    def first(src, dst, to_y, send, recv):
        is_self = jnp.logical_and(to_y == y, h == core)

        def copy(dz):
            return remote(src, dst, send.at[dz], recv, dev(to_y, x, (z + dz) % 8, h))

        def start():
            for dz in (1, 7, 2, 6, 3, 5, 4):
                copy(dz).start()

            @pl.when(is_self)
            def _():
                pltpu.make_async_copy(src, dst, recv).start()

            @pl.when(jnp.logical_not(is_self))
            def _():
                copy(0).start()

        def done():
            for dz in range(1, 8):
                wait_bytes(src, send.at[dz])

            @pl.when(jnp.logical_not(is_self))
            def _():
                wait_bytes(src, send.at[0])

        return start, done

    bc_start, bc_done = first(bst, bcs.at[zc, core], y, bsend, brecv.at[zc, core])
    zx_start, zx_done = first(zx, own_z(inner_side, ys, zl, core), y_to, zsend, zrecv.at[inner_side, zl, core])
    bc_start()
    zx_start()
    merge = remote(ow, ows.at[core], swap_s.at[2], swap_r.at[2], partner)
    merge.start()
    merge_own = pltpu.make_async_copy(ow, ows.at[core], local.at[2])
    merge_own.start()
    tok_own = pltpu.make_async_copy(tok, xs.at[core], local.at[0])
    tok_own.start()
    tok_far = remote(tok, xs.at[core], swap_s.at[0], swap_r.at[0], partner)
    tok_far.start()

    def view_b(half, sy, sx, part):
        lanes = pl.ds(1024 * half, 1024) if part is None else pl.ds(1024 * half + 512 * part, 512)
        return wb.at[sy, core, sx % 2, sx // 2, :, lanes]

    def view_g(g):
        def view(half, sy, sx, part):
            rows = pl.ds(0, 32) if part is None else pl.ds(16 * part, 16)
            return wz.at[g, sy, sx % 2, half, sx // 2, rows]

        return view

    my_lanes = pl.multiple_of(1024 * core, 1024)

    my_lanes = pl.multiple_of(1024 * core, 1024)
    far_lanes = pl.multiple_of(1024 * (1 - core), 1024)

    def view_o1(half, sy, sx, part):
        size = 256 if half else PLANE_FIRST - 256
        base = my_lanes + half * (PLANE_FIRST - 256)
        lanes = pl.ds(base, size) if part is None else pl.ds(base + size // 2 * part, size // 2)
        return wo.at[sy, sx % 2, z, sx // 2, :, lanes]

    def view_o2(half, sy, sx, part):
        zs = pl.ds(0, 8) if part is None else pl.ds(4 * part, 4)
        return wo.at[sy, sx % 2, zs, sx // 2, :, pl.ds(my_lanes + PLANE_FIRST, 1024 - PLANE_FIRST)]

    def plane(zsrc, part, base=None):
        return wo.at[:, :, zsrc, :, :, pl.ds((my_lanes if base is None else base) + PLANE_FIRST // 2 * part, PLANE_FIRST // 2)]

    def corner(j, base):
        sx = (x - j) % 4
        return wo.at[:, sx % 2, :, sx // 2, :, pl.ds(base + PLANE_FIRST, 1024 - PLANE_FIRST)]

    o_copies = []

    def o_send(zsrc, way, d, part):
        ref = plane(zsrc, part)
        to = dev(y, x, (z + 1 + 6 * way) % 8, core)
        cp = remote(ref, ref, ozs.at[way, d, part], ozr.at[way, d, part], to)
        cp.start()
        o_copies.append(cp)

    def o_hand(ref, index):
        cp = remote(ref, ref, osw_s.at[index], osw_r.at[index], partner)
        cp.start()
        o_copies.append(cp)

    def o_swap(zsrc, d):
        for part in range(2):
            o_hand(plane(zsrc, part), 2 * d + part)

    def o_turn(d):
        for way in range(2):
            zsrc = (z - d) % 8 if way == 0 else (z + d) % 8
            for part in range(2):
                if d < 4 or part == way:
                    wait_bytes(plane(zsrc, part), ozr.at[way, d - 1, part])
                if d < 3 or (d == 3 and part == way):
                    o_send(zsrc, way, d, part)
        for way in range(2):
            zsrc = (z - d) % 8 if way == 0 else (z + d) % 8
            if d < 4 or way == 0:
                o_swap(zsrc, d if way == 0 else 8 - d)

    same = lambda v: v
    flip = lambda v: (v + 2) % 4
    set_b = Ring(view_b, same, gs.at[0], gr.at[0])
    set_i = Ring(view_g(1), same, gs.at[1], gr.at[1])
    set_g = Ring(view_g(0), flip, gs.at[2], gr.at[2])
    set_o = Ring(view_o1, same, gs.at[3], gr.at[3])
    set_p = Ring(view_o2, same, gs.at[4], gr.at[4], (1,))

    merge_own.wait()
    wait_bytes(ows.at[1 - core], swap_r.at[2])
    for s in range(2):
        v = ows[s].astype(F32)
        for j in range(2):
            owf[8 * s : 8 * s + 8, 1024 * j : 1024 * j + 1024] = v[8 * j : 8 * j + 8, :]
    owm[...] = owf[...].astype(BF16)
    own_lanes = pl.ds(my_lanes, 1024)
    put = pltpu.make_async_copy(owm.at[:, own_lanes], wo.at[y, xl, z, xh, :, own_lanes], local.at[2])
    put.start()
    put.wait()
    set_o.begin()

    tok_own.wait()
    wait_bytes(xs.at[1 - core], swap_r.at[0])
    raw = dot_nt(xs[...].reshape(ROWS, 2048), dtw[...]).astype(BF16)
    row = lax.broadcasted_iota(jnp.int32, (64, 32), 0)
    col = lax.broadcasted_iota(jnp.int32, (64, 32), 1)
    pick = row == head_map(core, (64, 32), 1) + 32 * (col // 16)
    v = dot_nn(raw, pick.astype(BF16))
    dt = jnp.maximum(v, 0.0) + jnp.log1p(jnp.exp(-jnp.abs(v)))
    dts[...] = dt

    def choose(ref):
        one = (lax.broadcasted_iota(jnp.int32, (32, 16), 0) == head_map(core, (32, 16), 1)).astype(BF16)
        wide_ref = jnp.broadcast_to(ref[...], (8, 32))
        return sum(dot_nn(p, one) for p in parts3(wide_ref))

    rate = choose(decay)
    skips = widen(choose(skip))
    rates = jnp.concatenate([rate, rate], axis=1)[:1]
    step = -dt * rates
    logdt = jnp.log(dt)
    r = lax.broadcasted_iota(jnp.int32, (BLOCK, BLOCK), 0)
    c = lax.broadcasted_iota(jnp.int32, (BLOCK, BLOCK), 1)
    lower = (c <= r).astype(BF16)
    upper = (c >= r).astype(BF16)
    fwd_col = lax.broadcasted_iota(jnp.int32, (BLOCK, 32), 1) < 16
    for b in range(NBLK):
        rows = slice(b * BLOCK, b * BLOCK + BLOCK)
        sp = parts3(step[rows])
        lam = jnp.where(fwd_col, sum(dot_nn(lower, p) for p in sp), sum(dot_nn(upper, p) for p in sp))
        lams[rows, :] = lam
        padded = jnp.concatenate([lam - logdt[rows], jnp.zeros((BLOCK, 96), F32)], axis=1)
        lamt[b] = jnp.transpose(padded)[:32]

    for d in range(2):
        cols = slice(16 * d, 16 * d + 16)
        for b in range(NBLK):
            rows = slice(b * BLOCK, b * BLOCK + BLOCK)
            lam = lams[rows, cols]
            end = lam[BLOCK - 1 : BLOCK] if d == 0 else lam[0:1]
            wide_f[d, rows, :] = widen(jnp.exp(end - lam) * dts[rows, cols])
            wl = widen(jnp.exp(lam))
            wide_l[d, rows, :] = wl
            dend[d, b] = wl[BLOCK - 1 : BLOCK] if d == 0 else wl[0:1]


    set_o.first()
    for q in range(4):
        for s in range(2):
            wait_bytes(bcs.at[q, s], brecv.at[q, s])
    for q in range(4):
        for s in range(2):
            v = bcs[q, s].astype(F32)
            for j in range(8):
                bcf[4 * q + 2 * s : 4 * q + 2 * s + 2, 256 * j : 256 * j + 256] = v[2 * j : 2 * j + 2, :]
    bcm[...] = bcf[...].astype(BF16)
    put = pltpu.make_async_copy(bcm, wb.at[y, core, xl, xh], local.at[1])
    put.start()
    put.wait()
    set_b.begin()
    for s in range(2):
        for q in range(2):
            wait_bytes(own_z(1, y, s, q), zrecv.at[1, s, q])
    set_i.begin()
    set_o.second()
    set_b.first()
    set_i.first()
    for j in (0, 1, 3, 2):
        set_o.third(j)
    for k in (1, 7, 2, 6, 3, 5, 4):
        ref = wo.at[y, xl, z, xh, :, pl.ds(my_lanes + PLANE_FIRST, 1024 - PLANE_FIRST)]
        cp = remote(ref, ref, o2s.at[k - 1], o2r.at[k - 1], dev(y, x, (z + k) % 8, core))
        cp.start()
        o_copies.append(cp)
    set_b.second()
    set_i.second()
    for j in range(4):
        set_o.fourth(j)
    for part in range(2):
        for way in range(2):
            o_send(z, way, 0, part)
    o_swap(z, 0)
    for j in (0, 1, 3, 2):
        set_b.third(j)
        set_i.third(j)
    for j in range(4):
        set_b.fourth(j)
    swaps = [remote(wb.at[:, core], wb.at[:, core], swap_s.at[1], swap_r.at[1], partner)]
    swaps[0].start()
    for s in range(2):
        for q in range(2):
            wait_bytes(own_z(0, flip(y), s, q), zrecv.at[0, s, q])
    set_g.begin()
    o_turn(1)
    wait_bytes(wb.at[:, 1 - core], swap_r.at[1])
    bco[...] = dot_nt(xs[...].reshape(ROWS, 2048), wb[...].reshape(512, 2048)).astype(BF16)

    def block_weights(b, carry):
        rows = pl.ds(pl.multiple_of(b * BLOCK, BLOCK), BLOCK)
        gf = dot_nt(bco[rows, 128:256], bco[rows, 0:128])
        gb = dot_nt(bco[rows, 384:512], bco[rows, 256:384])
        g = jnp.where(r > c, gf, jnp.where(r < c, gb, 0.0))
        lam = lams[rows, :]
        lt = lamt[b]
        for lh in range(16):
            gap_f = lam[:, lh : lh + 1] - lt[lh : lh + 1, :]
            gap_b = lam[:, 16 + lh : 17 + lh] - lt[16 + lh : 17 + lh, :]
            w = g * jnp.exp(jnp.where(r > c, gap_f, gap_b))
            wm[b, :, 128 * lh : 128 * lh + 128] = w.astype(BF16)
        return carry

    lax.fori_loop(0, NBLK, block_weights, 0)

    for j in range(4):
        set_i.fourth(j)
    for g in range(4):
        w = wz[1, g].reshape(256, 2048)
        inner[:, 256 * g : 256 * g + 256] = dot_nt(xs[...].reshape(ROWS, 2048), w).astype(BF16)

    def send_states(src, dst, ss, rs):
        cs = []
        for k in (8, 7, 9, 6, 10, 5, 11, 4, 12, 3, 13, 2, 14, 1, 15):
            j = (chip + k) % 16
            c = remote(src.at[j], dst.at[chip], ss.at[k - 1], rs.at[k - 1], state_peer(j))
            c.start()
            cs.append(c)
        dst[pl.ds(chip, 1)] = src[pl.ds(chip, 1)]
        return cs

    def wait_states(dst, rs):
        for k in range(1, 16):
            wait_bytes(dst.at[(chip - k) % 16], rs.at[k - 1])

    both_decays = []
    for d in range(2):
        decays = dend[d, 0]
        for b in range(1, NBLK):
            decays = decays * dend[d, b]
        both_decays += [p.astype(F32) for p in parts3(decays)]
    tail = jnp.concatenate(both_decays + [jnp.zeros((10, WIDE), F32)], axis=0).astype(BF16)
    state_copies = []
    for d in range(2):
        pay = (pay_f, pay_b)[d]
        state = jnp.zeros((BLOCK, WIDE), F32)
        for b in range(NBLK) if d == 0 else reversed(range(NBLK)):
            rows = slice(b * BLOCK, b * BLOCK + BLOCK)
            scaled = (wide_f[d, rows, :] * inner[rows, :].astype(F32)).astype(BF16)
            k = dot_tn(bco[rows, 256 * d : 256 * d + 128], scaled)
            kst[d, b] = k
            state = dend[d, b] * state + k
        for j in range(16):
            q, nh = j // 2, j % 2
            pay[j, :64, :] = state[64 * nh : 64 * nh + 64, 128 * q : 128 * q + 128].astype(BF16)
            if d == 0:
                pay[j, 64:80, :] = tail[:, 128 * q : 128 * q + 128]
        state_copies += send_states(pay, (got_f, got_b)[d], s1.at[d], r1.at[d])
    set_g.first()
    o_turn(2)
    set_g.second()
    for k in range(1, 8):
        lanes = pl.ds(my_lanes + PLANE_FIRST, 1024 - PLANE_FIRST)
        wait_bytes(wo.at[y, xl, (z - k) % 8, xh, :, lanes], o2r.at[k - 1])
    set_p.begin()
    set_g.third(0)

    left = lax.broadcasted_iota(jnp.int32, (BLOCK, BLOCK), 1) < 64

    def block_intra(b, carry):
        rows = pl.ds(pl.multiple_of(b * BLOCK, BLOCK), BLOCK)
        for q in range(8):
            pair = inner[rows, 128 * q : 128 * q + 128]
            zero = jnp.zeros_like(pair)
            stack = jnp.concatenate([jnp.where(left, pair, zero), jnp.where(left, zero, pair)], axis=0)
            out = dot_nn(wm[b, :, 256 * q : 256 * q + 256], stack)
            yo[rows, 128 * q : 128 * q + 128] = out + skips[:1, 128 * q : 128 * q + 128] * pair.astype(F32)
        return carry

    lax.fori_loop(0, NBLK, block_intra, 0)

    for d in range(2):
        got = (got_f, got_b)[d]
        wait_states(got, r1.at[d])
        state = jnp.zeros((64, 128), F32)
        for i in range(16) if d == 0 else reversed(range(16)):
            reply[d, i] = state.astype(BF16)
            ds = got_f[i, 64:80, :].astype(F32)
            de = ds[3 * d : 3 * d + 1] + ds[3 * d + 1 : 3 * d + 2] + ds[3 * d + 2 : 3 * d + 3]
            state = de * state + got[i, :64, :].astype(F32)
        state_copies += send_states(reply.at[d], ent.at[d], s2.at[d], r2.at[d])
        if d == 0:
            for j in (1, 3, 2):
                set_g.third(j)
    set_p.first()
    set_p.second()
    o_turn(3)
    for j in range(4):
        set_g.fourth(j)
    for g in range(4):
        w = wz[0, g].reshape(256, 2048)
        gate = dot_nt(xs[...].reshape(ROWS, 2048), w).astype(BF16).astype(F32)
        wide_f[0, :, 256 * g : 256 * g + 256] = gate / (1.0 + jnp.exp(-gate))
    for j in (0, 1, 3, 2):
        set_p.third(j)
    for d in range(2):
        wait_states(ent.at[d], r2.at[d])
        for q in range(8):
            cols = slice(128 * q, 128 * q + 128)
            for nh in range(2):
                enter[64 * nh : 64 * nh + 64, cols] = ent[d, 2 * q + nh].astype(F32)
        state = enter[...]
        for b in range(NBLK) if d == 0 else reversed(range(NBLK)):
            rows = slice(b * BLOCK, b * BLOCK + BLOCK)
            cv = bco[rows, 256 * d + 128 : 256 * d + 256]
            yo[rows, :] = yo[rows, :] + wide_l[d, rows, :] * dot_nn(cv, state.astype(BF16))
            state = dend[d, b] * state + kst[d, b]

    theirs = pl.ds(pl.multiple_of((1 - core) * 256, 256), 256)
    mine = pl.ds(pl.multiple_of(core * 256, 256), 256)
    squares = jnp.zeros((ROWS, 1), F32)
    pair_copies = []
    for g in range(4):
        cols = slice(256 * g, 256 * g + 256)
        gated = yo[:, cols] * wide_f[0, :, cols]
        squares = squares + jnp.sum(gated * gated, axis=1, keepdims=True)
        for i in range(2 * g, 2 * g + 2):
            place = pl.ds(natural(core, i), 128)
            cols = slice(128 * i, 128 * i + 128)
            part = gated[:, 128 * (i % 2) : 128 * (i % 2) + 128]
            gbuf[:, cols] = (part * gain[0:1, place]).astype(BF16)
            cp = remote(gbuf.at[theirs, cols], wide.at[:, place], ps.at[i], pr.at[i], partner)
            cp.start()
            pair_copies.append(cp)
            wide[:, place] = gbuf[mine, cols]
    sqb[...] = jnp.broadcast_to(squares, (ROWS, 128))
    cp = remote(sqb.at[theirs], sqf, ps.at[8], pr.at[8], partner)
    cp.start()
    pair_copies.append(cp)

    o_turn(4)
    for j in (0, 1, 3, 2):
        set_p.fourth(j)
        o_hand(corner(j, my_lanes), 16 + j)
    for i in range(8):
        wait_bytes(wide.at[:, pl.ds(natural(1 - core, i), 128)], pr.at[i])
    wait_bytes(sqf, pr.at[8])
    scale = lax.rsqrt((sqb[mine, :1] + sqf[:, :1]) * (1.0 / 2048.0) + 1e-05)
    for d in range(8):
        for part in range(2):
            wait_bytes(plane((z - d) % 8, part, far_lanes), osw_r.at[2 * d + part])
    for j in range(4):
        wait_bytes(corner(j, far_lanes), osw_r.at[16 + j])
    for g in range(8):
        w = wo[g // 2, g % 2].reshape(256, 2048)
        result[:, 256 * g : 256 * g + 256] = (dot_nt(wide[...], w) * scale).astype(BF16)

    bc_done()
    zx_done()
    for s in (set_b, set_i, set_g, set_o, set_p):
        s.drain()
    tok_far.wait_send()
    merge.wait_send()
    for cp in swaps + state_copies + pair_copies + o_copies:
        cp.wait_send()


ANY = pl.BlockSpec(memory_space=pl.ANY)
INV = pl.BlockSpec(memory_space=pltpu.VMEM)


def layer(zx, bc, ow, tok, dtw, decay, skip, gain):
    dma = pltpu.SemaphoreType.DMA
    vm = pltpu.VMEM
    return pl.pallas_call(
        kernel,
        out_shape=jax.ShapeDtypeStruct((256, 2048), BF16),
        in_specs=[ANY, INV, ANY, ANY, INV, INV, INV, INV],
        out_specs=INV,
        scratch_shapes=[
            vm((2, 4, 2, 2, 2, 32, 2048), BF16), vm((4, 2, 2, 2, 16, 2048), BF16),
            vm((4, 2, 8, 2, 16, 2048), BF16), vm((2, 256, 2048), BF16),
            vm((16, 256), BF16), vm((16, 256), F32),
            vm((4, 2, 16, 256), BF16), vm((2, 16, 1024), BF16),
            vm((16, 2048), BF16), vm((16, 2048), F32), vm((16, 2048), BF16), vm((16, 2048), F32),
            vm((ROWS, WIDE), BF16), vm((ROWS, 512), BF16), vm((ROWS, 32), F32), vm((ROWS, 32), F32),
            vm((NBLK, 32, BLOCK), F32), vm((2, ROWS, WIDE), F32), vm((2, ROWS, WIDE), F32),
            vm((NBLK, BLOCK, 2048), BF16), vm((2, NBLK, BLOCK, WIDE), F32), vm((2, NBLK, 1, WIDE), F32),
            vm((ROWS, WIDE), F32), vm((BLOCK, WIDE), F32),
            vm((16, 80, 128), BF16), vm((16, 64, 128), BF16), vm((16, 80, 128), BF16), vm((16, 64, 128), BF16),
            vm((2, 16, 64, 128), BF16), vm((2, 16, 64, 128), BF16), vm((ROWS, WIDE), BF16), vm((256, 2048), BF16),
            vm((ROWS, 128), F32), vm((256, 128), F32),
            dma((8,)), dma((2, 2, 2)), dma((8,)), dma((4, 2)), dma((3,)), dma((5, 2, 20)), dma((5, 2, 20)),
            dma((2, 4, 2)), dma((2, 4, 2)), dma((24,)), dma((24,)), dma((7,)), dma((7,)), dma((3,)), dma((3,)),
            dma((2, 15)), dma((2, 15)), dma((2, 15)), dma((2, 15)), dma((9,)), dma((9,)),
        ],
        compiler_params=pltpu.CompilerParams(
            collective_id=0, has_side_effects=True, vmem_limit_bytes=VMEM_BYTES
        ),
        name="layer",
    )(zx, bc, ow, tok, dtw, decay, skip, gain)


def shards(tokens, zx_weight, bc_weight, dt_weight, decay_rate, skip_gain, norm_gain, out_weight):
    ow = out_weight.T.reshape(8, 2, 1024).transpose(1, 0, 2).reshape(16, 1024)
    return layer(
        zx_weight.T, bc_weight.T, ow, tokens[0], dt_weight.T,
        decay_rate[None], skip_gain[None], norm_gain[None],
    )[None]


def solution(mesh):
    columns = P(None, ("fsdp", "ctx"))
    in_specs = (P("fsdp", "ctx", None), columns, columns, P(), P(), P(), P(), columns)
    return jax.shard_map(
        shards, mesh=mesh, in_specs=in_specs, out_specs=P("fsdp", "ctx", None), check_vma=False
    )
```
